256 devices in a mesh: row: 16 (over y, z_lo, core), sample: 16 (over z_hi, x).
Axes of the slice: x: 4, y: 4, z: 8 (z_hi: 4, z_lo: 2; z = z_hi * 2 + z_lo), core: 2. Of those that a mesh axis runs over, the one named last changes fastest.
Arguments:
- atom_feat: bfloat16 [32, 18432, 128], P('sample', 'row'), may hold values from -24 to 24
- atom_token: int32 [18432], P('row'), may hold values from 0 to 1151, as said below
- pair_cond: bfloat16 [1152, 1152, 128], P('row', 'sample'), may hold values from -24 to 24
- token_mask: int32 [1152], P('sample'), may hold values 0 or 1
- atom_wq: bfloat16 [128, 128], replicated, may hold values from -3 to 3
- atom_wk: bfloat16 [128, 128], replicated, may hold values from -3 to 3
- atom_wv: bfloat16 [128, 128], replicated, may hold values from -0.5 to 0.5
- atom_wo: bfloat16 [128, 128], replicated, may hold values from -0.5 to 0.5
- agg_weight: bfloat16 [128, 768], replicated, may hold values from -0.5 to 0.5
- pair_weight: bfloat16 [128, 16], replicated, may hold values from -64 to 64
- token_gain: float32 [768], replicated, may hold values from 0.5 to 1.5
- query_weight: bfloat16 [768, 768], replicated, may hold values from -0.21875 to 0.21875
- key_weight: bfloat16 [768, 768], replicated, may hold values from -0.21875 to 0.21875
- value_weight: bfloat16 [768, 768], replicated, may hold values from -0.21875 to 0.21875
- gate_weight: bfloat16 [768, 768], replicated, may hold values from -0.21875 to 0.21875
- out_weight: bfloat16 [768, 768], replicated, may hold values from -0.21875 to 0.21875
Outputs:
- token_out: bfloat16 [32, 1152, 768], P('sample', 'row')
The draws below stay inside these ranges and needn't reach their ends.
Inputs may be any that keep to these rules, and one draw needn't show every extreme that they name: atom_token never falls along the atoms; atoms 1152 r to 1152 (r + 1) - 1 belong to tokens 72 r to 72 (r + 1) - 1, and every token has at least one atom.
All inputs are finite; a program needn't handle non-finite values. No bound on the sum of `token_mask` on one device may be relied on, other than what follows from the above.
Results may differ from the reference program's by a relative error of at most 0.008.
The reference program's roundings to bfloat16 on the way count: a program that leaves them out, or rounds other values in their place, can miss the bound.
Values may be sent and summed in bfloat16 or wider, within the bound.
A program may use at most 128 MiB of HBM per device.

```python
import jax
import jax.numpy as jnp
from jax import lax

D = 768
HEADS = 16
HEAD_DIM = 48
CZ = 128
CA = 128
AHEADS = 4
AHEAD_DIM = 32
QWIN = 32
KWIN = 128
TOK_ROW = 72
ATOM_DEV = 1152
SAMPLES = 32
NTOK = 1152
NATOM = 18432


def draw_atom_token(key, part):
    key = jax.random.fold_in(key, 11)
    blocks = NATOM // ATOM_DEV
    extra = jax.random.randint(key, (blocks, ATOM_DEV - TOK_ROW), 0, TOK_ROW, dtype=jnp.int32)
    first = jnp.broadcast_to(jnp.arange(TOK_ROW, dtype=jnp.int32)[None, :], (blocks, TOK_ROW))
    local = jnp.sort(jnp.concatenate([first, extra], axis=1), axis=1)
    offset = (jnp.arange(blocks, dtype=jnp.int32) * TOK_ROW)[:, None]
    return (local + offset).reshape(-1).astype(jnp.int32)


def draw_atom_feat(key, part):
    key = jax.random.fold_in(key, 21)
    noise_key = jax.random.fold_in(key, 0)
    base_noise = jnp.clip(jax.random.normal(noise_key, (SAMPLES, NATOM, CA), jnp.float32), -6.0, 6.0)
    return base_noise.astype(jnp.bfloat16)


def draw_atom_wq(key, part):
    key = jax.random.fold_in(key, 22)
    drawn_part = jnp.clip(jax.random.normal(key, (CA, CA), jnp.float32), -6.0, 6.0) / CA ** 0.5
    return drawn_part.astype(jnp.bfloat16)


def draw_atom_wk(key, part):
    key = jax.random.fold_in(key, 23)
    drawn_part = jnp.clip(jax.random.normal(key, (CA, CA), jnp.float32), -6.0, 6.0) / CA ** 0.5
    return drawn_part.astype(jnp.bfloat16)


def draw_pair_cond(key, part):
    key = jax.random.fold_in(key, 24)
    noise_key = jax.random.fold_in(key, 0)
    base_noise = jnp.clip(jax.random.normal(noise_key, (NTOK, NTOK, CZ), jnp.float32), -6.0, 6.0)
    return base_noise.astype(jnp.bfloat16)


def draw_pair_weight(key, part):
    key = jax.random.fold_in(key, 25)
    drawn_part = jnp.clip(jax.random.normal(key, (CZ, HEADS), jnp.float32), -6.0, 6.0) / CZ ** 0.5
    return drawn_part.astype(jnp.bfloat16)


def plant(drawn, stream_key, low, largest):
    index_at = [jax.random.randint(jax.random.fold_in(stream_key, axis), (), 0, length) for axis, length in enumerate(drawn.shape)]
    main_axis = drawn.shape.index(max(drawn.shape))
    next_to = index_at[:main_axis] + [(index_at[main_axis] + 1) % drawn.shape[main_axis]] + index_at[main_axis + 1:]
    return drawn.at[tuple(index_at)].set(low).at[tuple(next_to)].set(largest)


def scatter_about(key, dims, scale, bound, kind=jnp.bfloat16):
    result = jax.random.normal(key, dims, jnp.float32) * scale
    return jnp.minimum(jnp.maximum(result, -bound), bound).astype(kind)


def setup_inputs(seed: int = 0) -> dict:
    streams_of = jax.random.split(jax.random.key(seed), 17)
    return {
        "atom_feat": draw_atom_feat(jax.random.fold_in(streams_of[16], 71), 0),
        "atom_token": draw_atom_token(jax.random.fold_in(streams_of[16], 71), 0),
        "pair_cond": draw_pair_cond(jax.random.fold_in(streams_of[16], 71), 0),
        "token_mask": plant((jax.random.randint(streams_of[3], (NTOK,), 0, 8) < 7).astype(jnp.int32), jax.random.fold_in(streams_of[3], 1), 0, 1),
        "atom_wq": draw_atom_wq(jax.random.fold_in(streams_of[16], 71), 0),
        "atom_wk": draw_atom_wk(jax.random.fold_in(streams_of[16], 71), 0),
        "atom_wv": scatter_about(streams_of[6], (CA, CA), CA ** -0.5, 0.5),
        "atom_wo": scatter_about(streams_of[7], (CA, CA), CA ** -0.5, 0.5),
        "agg_weight": scatter_about(streams_of[8], (CA, D), CA ** -0.5, 0.5),
        "pair_weight": draw_pair_weight(jax.random.fold_in(streams_of[16], 71), 0),
        "token_gain": jnp.clip(1.0 + 0.1 * jax.random.normal(streams_of[10], (D,), jnp.float32), 0.5, 1.5),
        "query_weight": scatter_about(streams_of[11], (D, D), D ** -0.5, 0.21875),
        "key_weight": scatter_about(streams_of[12], (D, D), D ** -0.5, 0.21875),
        "value_weight": scatter_about(streams_of[13], (D, D), D ** -0.5, 0.21875),
        "gate_weight": scatter_about(streams_of[14], (D, D), D ** -0.5, 0.21875),
        "out_weight": scatter_about(streams_of[15], (D, D), D ** -0.5, 0.21875),
    }


def layer_norm(x):
    mean = lax.optimization_barrier(jnp.mean(x, -1, keepdims=True))
    centre = x - mean
    var = lax.optimization_barrier(jnp.mean(centre * centre, -1, keepdims=True))
    return centre * lax.rsqrt(var + 1e-05)

def reference(atom_feat, atom_token, pair_cond, token_mask, atom_wq, atom_wk, atom_wv, atom_wo, agg_weight, pair_weight, token_gain, query_weight, key_weight, value_weight, gate_weight, out_weight):
    rim = (KWIN - QWIN) // 2
    windows = NATOM // QWIN
    ascale = 1.0 / AHEAD_DIM ** 0.5
    tscale = 1.0 / HEAD_DIM ** 0.5

    def bias_row(pair_row):
        normed = layer_norm(pair_row.astype(jnp.float32)).astype(jnp.bfloat16)
        return jnp.dot(normed, pair_weight, preferred_element_type=jnp.float32)
    bias_raw = lax.map(bias_row, pair_cond)
    qidx = jnp.arange(NTOK, dtype=jnp.int32)
    allowed = (token_mask[None, :] == 1) | (qidx[:, None] == qidx[None, :])
    bias = jnp.where(allowed[:, :, None], bias_raw, -30000.0).astype(jnp.bfloat16)
    bias = jnp.transpose(bias, (2, 0, 1))
    counts = jax.ops.segment_sum(jnp.ones((NATOM,), jnp.float32), atom_token, NTOK)
    wid = jnp.arange(windows, dtype=jnp.int32)
    tid = jnp.arange(KWIN, dtype=jnp.int32)
    gidx = wid[:, None] * QWIN - rim + tid[None, :]
    valid = (gidx >= 0) & (gidx < NATOM)

    def one_sample(feat):
        normed = layer_norm(feat.astype(jnp.float32)).astype(jnp.bfloat16)
        atom_q = jnp.dot(normed, atom_wq, preferred_element_type=jnp.float32).astype(jnp.bfloat16)
        atom_k = jnp.dot(normed, atom_wk, preferred_element_type=jnp.float32).astype(jnp.bfloat16)
        atom_v = jnp.dot(normed, atom_wv, preferred_element_type=jnp.float32).astype(jnp.bfloat16)
        atom_k = jnp.pad(atom_k, ((rim, rim), (0, 0))).reshape(windows + 3, QWIN, CA)
        atom_v = jnp.pad(atom_v, ((rim, rim), (0, 0))).reshape(windows + 3, QWIN, CA)
        atom_k = jnp.concatenate([atom_k[k:k + windows] for k in range(4)], axis=1).reshape(windows, KWIN, AHEADS, AHEAD_DIM)
        atom_v = jnp.concatenate([atom_v[k:k + windows] for k in range(4)], axis=1).reshape(windows, KWIN, AHEADS, AHEAD_DIM)
        atom_q = atom_q.reshape(windows, QWIN, AHEADS, AHEAD_DIM)
        scores = jnp.einsum('wqhd,wkhd->whqk', atom_q.astype(jnp.float32), atom_k.astype(jnp.float32)) * ascale
        scores = jnp.where(valid[:, None, None, :], scores, -jnp.inf)
        atom_e = jnp.exp(scores - lax.optimization_barrier(jnp.max(scores, -1, keepdims=True)))
        atom_l = lax.optimization_barrier(jnp.sum(atom_e, -1))
        mixed = jnp.einsum('whqk,wkhd->whqd', atom_e.astype(jnp.bfloat16).astype(jnp.float32), atom_v.astype(jnp.float32)) / atom_l[..., None]
        mixed = jnp.transpose(mixed, (0, 2, 1, 3)).reshape(NATOM, CA).astype(jnp.bfloat16)
        atom_out = (feat.astype(jnp.float32) + jnp.dot(mixed, atom_wo, preferred_element_type=jnp.float32)).astype(jnp.bfloat16)
        hidden = jax.nn.relu(jnp.dot(atom_out, agg_weight, preferred_element_type=jnp.float32)).astype(jnp.bfloat16)
        token_in = jax.ops.segment_sum(hidden.astype(jnp.float32), atom_token, NTOK) / counts[:, None]
        tnorm = (layer_norm(token_in) * token_gain).astype(jnp.bfloat16)
        tq = jnp.dot(tnorm, query_weight, preferred_element_type=jnp.float32).astype(jnp.bfloat16).reshape(NTOK, HEADS, HEAD_DIM)
        tk = jnp.dot(tnorm, key_weight, preferred_element_type=jnp.float32).astype(jnp.bfloat16).reshape(NTOK, HEADS, HEAD_DIM)
        tv = jnp.dot(tnorm, value_weight, preferred_element_type=jnp.float32).astype(jnp.bfloat16).reshape(NTOK, HEADS, HEAD_DIM)
        gate = jnp.dot(tnorm, gate_weight, preferred_element_type=jnp.float32)
        tscores = jnp.einsum('qhd,khd->hqk', tq.astype(jnp.float32), tk.astype(jnp.float32)) * tscale + bias.astype(jnp.float32)
        tok_e = jnp.exp(tscores - lax.optimization_barrier(jnp.max(tscores, -1, keepdims=True)))
        tok_l = lax.optimization_barrier(jnp.sum(tok_e, -1))
        tmix = jnp.einsum('hqk,khd->hqd', tok_e.astype(jnp.bfloat16).astype(jnp.float32), tv.astype(jnp.float32)) / tok_l[..., None]
        tmix = jnp.transpose(tmix, (1, 0, 2)).reshape(NTOK, D)
        gated = (tmix * jax.nn.sigmoid(gate)).astype(jnp.bfloat16)
        return (token_in + jnp.dot(gated, out_weight, preferred_element_type=jnp.float32)).astype(jnp.bfloat16)
    return lax.map(one_sample, atom_feat)
```

```python
import jax
import jax.numpy as jnp
from jax import lax
from jax.experimental import pallas as pl
from jax.experimental.pallas import tpu as pltpu
from jax.sharding import PartitionSpec as P

HEADS = 16
HEAD_DIM = 48
AHEADS = 4
AHEAD_DIM = 32
QWIN = 32
KWIN = 128
RIM = 48
TOK = 72
PAD = 80
ATOMS = 1152
CA = 128
D = 768
LANES = HEADS * TOK
F32 = jnp.float32
BF16 = jnp.bfloat16
NEG = -1e30
CHUNKS = ((0, 256, 0, 256), (256, 256, 128, 256), (512, 256, 256, 384), (768, 256, 384, 384), (1024, 128, 640, 128))


def dot(a, b):
    return jnp.dot(a, b, preferred_element_type=F32)


def dot_nt(a, b):
    return lax.dot_general(a, b, (((1,), (1,)), ((), ())), preferred_element_type=F32)


def layer_norm(x):
    mean = jnp.mean(x, -1, keepdims=True)
    centre = x - mean
    var = jnp.mean(centre * centre, -1, keepdims=True)
    return centre * lax.rsqrt(var + 1e-05)


def iota(shape, dim):
    return lax.broadcasted_iota(jnp.int32, shape, dim)


MESH = pl.DeviceIdType.MESH
KEYS = 16 * PAD
HALF = 8 * PAD
PARTS = ((0, 48), (48, 32))


def pair_part(pair_ref, mask_ref, weight_ref, table_ref, out, row, col, unroll=12):
    weight_t = weight_ref[...]

    def step(g, carry):
        normed = [layer_norm(pair_ref[g * unroll + u].astype(F32)).astype(BF16) for u in range(unroll)]
        raw = [dot_nt(weight_t, n) for n in normed]
        for u in range(unroll):
            table_ref[pl.ds(g * unroll + u, HEADS, stride=TOK), :TOK] = raw[u]
        return carry

    lax.fori_loop(0, TOK // unroll, step, 0)
    kidx = col * TOK + iota((TOK, TOK), 1)
    qidx = row * TOK + iota((TOK, TOK), 0)
    allowed = (mask_ref[...] == 1) | (qidx == kidx)
    for h in range(HEADS):
        rows = pl.ds(h * TOK, TOK)
        table_ref[rows, :TOK] = jnp.where(allowed, table_ref[rows, :TOK], -30000.0)
    for n in range(LANES // 128):
        part = table_ref[n * 128 : (n + 1) * 128, :].T[:TOK]
        filled = jnp.concatenate([part, jnp.full((PAD - TOK, 128), NEG, F32)], axis=0)
        out[:, n * 128 : (n + 1) * 128] = filled.astype(BF16)


def atom_project(s, halo_ref, feat_ref, wq, wk, wv, normed_ref, q_ref, k_ref, v_ref, row, rows):
    def norm_step(start, source):
        normed_ref[pl.ds(start, source.shape[0]), :] = layer_norm(source.astype(F32)).astype(BF16)

    norm_step(0, halo_ref[0, s])
    norm_step(RIM + ATOMS, halo_ref[1, s])
    for c in range(9):
        norm_step(RIM + c * 128, feat_ref[s, c * 128 : (c + 1) * 128])
    for c in range(3):
        here = pl.ds(c * 416, 416)
        block = normed_ref[here, :]
        k_ref[here, :] = dot(block, wk).astype(BF16)
        v_ref[here, :CA] = dot(block, wv).astype(BF16)
        v_ref[here, CA:] = jnp.ones((416, CA), BF16)
        q_ref[pl.ds(c * 384, 384), :] = dot(normed_ref[pl.ds(RIM + c * 384, 384), :], wq).astype(BF16)
    last = RIM + ATOMS
    first_key = k_ref[RIM : RIM + 16, :].astype(F32)[:1]
    last_key = k_ref[last - 16 : last, :].astype(F32)[15:]
    for outside, start, key in ((row == 0, 0, first_key), (row == rows - 1, last, last_key)):
        here = pl.ds(start, RIM)
        k_ref[here, :] = jnp.where(outside, jnp.broadcast_to(key, (RIM, CA)), k_ref[here, :].astype(F32)).astype(BF16)
        v_ref[here, :] = jnp.where(outside, 0.0, v_ref[here, :].astype(F32)).astype(BF16)


def atom_windows(q_ref, k_ref, v_ref, att_ref, first, group=12):
    head_of = iota((AHEADS * QWIN, CA), 0) // QWIN == iota((AHEADS * QWIN, CA), 1) // AHEAD_DIM
    lane_head = iota((QWIN, CA), 1) // AHEAD_DIM
    factor = 1.4426950408889634 / AHEAD_DIM**0.5
    starts = [pl.multiple_of(first + u * QWIN, QWIN) for u in range(group)]
    scores = []
    for start in starts:
        q = q_ref[pl.ds(start, QWIN), :]
        stacked = jnp.where(head_of, jnp.concatenate([q] * AHEADS, axis=0), jnp.zeros((), BF16))
        scores.append(dot_nt(stacked, k_ref[pl.ds(start, KWIN), :]))
    exps = [jnp.exp2((sc - jnp.max(sc, -1, keepdims=True)) * factor).astype(BF16) for sc in scores]
    for start, e in zip(starts, exps):
        both = dot(e, v_ref[pl.ds(start, KWIN), :])
        top, low = both[:QWIN, :CA], both[:QWIN, CA:]
        for h in range(1, AHEADS):
            here = slice(h * QWIN, (h + 1) * QWIN)
            top = jnp.where(lane_head == h, both[here, :CA], top)
            low = jnp.where(lane_head == h, both[here, CA:], low)
        att_ref[pl.ds(start, QWIN), :] = (top / low).astype(BF16)


def atom_tokens(s, feat_ref, token_ref, wo, agg_ref, gain_ref, att_ref, token_in_ref, row):
    total = jnp.zeros((TOK, D), F32)
    counts = jnp.zeros((TOK, 1), F32)
    for c in range(3):
        here = pl.ds(c * 384, 384)
        out = (feat_ref[s, here, :].astype(F32) + dot(att_ref[here, :], wo)).astype(BF16)
        hidden = jnp.maximum(dot(out, agg_ref[...]), 0.0).astype(BF16)
        onehot = token_ref[:, c * 384 : (c + 1) * 384] - row * TOK == iota((TOK, 384), 0)
        total += dot(onehot.astype(BF16), hidden)
        counts += jnp.sum(onehot.astype(F32), -1, keepdims=True)
    token_in = total / counts
    token_in_ref[s] = token_in
    tnorm = layer_norm(token_in) * gain_ref[...]
    return jnp.concatenate([tnorm, jnp.zeros((PAD - TOK, D), F32)], axis=0).astype(BF16)


def query_prep(qt_ref, slab, chunk):
    lo, width, clo, cwidth = chunk
    lane = lo + iota((TOK, width), 1)
    fold = (lane % TOK == iota((TOK, width), 0)).astype(BF16)
    own_head = (lo + iota((cwidth, width), 1)) // TOK == (clo + iota((cwidth, width), 0)) // HEAD_DIM
    query = jnp.where(own_head, dot(qt_ref[slab, pl.ds(clo, cwidth), :], fold), 0.0).astype(BF16)
    return fold, own_head, query


def attend(k_ref, vt_ref, bias_of, qt_ref, scores_ref, p_ref, mix_ref, after_slab, blk=PAD * 2):
    mix_ref[...] = jnp.zeros_like(mix_ref)
    work = [(slab, chunk) for slab in range(2) for chunk in CHUNKS]
    blocks = KEYS // blk
    state = {}
    for i in range(len(work) + 2):
        now = work[i] if i < len(work) else None
        exps = work[i - 1] if 0 <= i - 1 < len(work) else None
        vals = work[i - 2] if i >= 2 else None
        if exps:
            top = jnp.max(state[i - 1][3], axis=0, keepdims=True)
            total = jnp.zeros((8, exps[1][1]), F32)
        if now:
            lo, width, clo, cwidth = now[1]
            state[i] = list(query_prep(qt_ref, *now)) + [jnp.full((8, width), -3e38, F32)]
            ahead = dot(k_ref[0:blk, clo : clo + cwidth], state[i][2])
        if vals:
            _, vwidth, vlo, vcwidth = vals[1]
            out = dot(vt_ref[pl.ds(vlo, vcwidth), :], p_ref[i % 2, :, :vwidth])
        for b in range(blocks):
            here = pl.ds(b * blk, blk)
            if now:
                raw = ahead
                if b + 1 < blocks:
                    ahead = dot(k_ref[(b + 1) * blk : (b + 2) * blk, clo : clo + cwidth], state[i][2])
            if exps:
                ewidth = exps[1][1]
                e = jnp.exp(scores_ref[(i - 1) % 2, here, :ewidth] - top)
                total += jnp.sum(e.reshape(blk // 8, 8, ewidth), axis=0)
                p_ref[(i - 1) % 2, here, :ewidth] = e.astype(BF16)
            if now:
                sc = raw * (1.0 / HEAD_DIM**0.5) + bias_of(now[0], b, blk, lo, width)
                scores_ref[i % 2, here, :width] = sc
                state[i][3] = jnp.maximum(state[i][3], jnp.max(sc.reshape(blk // 8, 8, width), axis=0))
        if exps:
            state[i - 1].append(jnp.sum(total, axis=0, keepdims=True))
        if vals:
            fold, own_head, _, _, vsum = state.pop(i - 2)
            out = jnp.where(own_head, out * (1.0 / vsum), 0.0)
            high = out.astype(BF16)
            rest = (out - high.astype(F32)).astype(BF16)
            mix_ref[vals[0], :, vlo : vlo + vcwidth] += dot_nt(fold, high) + dot_nt(fold, rest)
            if vals[1] is CHUNKS[-1]:
                after_slab(vals[0])


def whole_kernel(pair_ref, mask_ref, pair_w_ref, feat_ref, token_ref, wq, wk, wv, wo, agg_ref, gain_ref,
                 query_hbm, key_hbm, value_hbm, gate_hbm, out_hbm, out_ref,
                 table_ref, halo_ref, normed_ref, q_ref, k_ref, v_ref, att_ref, token_in_ref, give_ref, tall_ref, bias_ref,
                 weights_ref, wvt_ref, keys_ref, vt_ref, qt_ref, sig_ref, scores_ref, p_ref, mix_ref, back_send, back_recv,
                 load_sem, halo_send, halo_recv, bias_send, bias_recv, twin_send, twin_recv, tok_send, tok_recv,
                 pass_send, pass_recv):
    row, col = lax.axis_index("row"), lax.axis_index("sample")
    rows, cols = lax.axis_size("row"), lax.axis_size("sample")
    core, zl, y = row % 2, (row // 2) % 2, row // 4
    x, zh = col % 4, col // 4
    twin, zpair = row + 1 - 2 * core, row + 2 - 4 * zl
    y_up, y_down = (row + 4) % rows, (row + rows - 4) % rows
    r_up, r_down = (row + 1) % rows, (row + rows - 1) % rows
    x_up, x_down = zh * 4 + (x + 1) % 4, zh * 4 + (x + 3) % 4
    z_up, z_down = (col + 4) % cols, (col + cols - 4) % cols
    loads = []
    for n, source in enumerate((query_hbm, key_hbm, value_hbm, gate_hbm, out_hbm)):
        loads.append(pltpu.make_async_copy(source, weights_ref.at[n], load_sem.at[n]))
        loads[-1].start()

    barrier = pltpu.get_barrier_semaphore()
    for peer in (twin, zpair, y_up, y_down, r_up, r_down):
        pl.semaphore_signal(barrier, inc=1, device_id=(peer, col), device_id_type=MESH)
    for peer in (x_up, x_down, z_up, z_down):
        pl.semaphore_signal(barrier, inc=1, device_id=(row, peer), device_id_type=MESH)
    pl.semaphore_wait(barrier, 10)

    sent = []

    def send(src, dst, send_sem, recv_sem, peer_row, peer_col):
        copy = pltpu.make_async_remote_copy(src_ref=src, dst_ref=dst, send_sem=send_sem, recv_sem=recv_sem,
                                            device_id=(peer_row, peer_col), device_id_type=MESH)
        copy.start()
        sent.append(copy)

    def wait(dst, send_sem, recv_sem, peer_row, peer_col):
        pltpu.make_async_remote_copy(src_ref=dst, dst_ref=dst, send_sem=send_sem, recv_sem=recv_sem,
                                     device_id=(peer_row, peer_col), device_id_type=MESH).wait_recv()

    send(feat_ref.at[:, ATOMS - RIM :], halo_ref.at[0], halo_send.at[0], halo_recv.at[0], r_up, col)
    send(feat_ref.at[:, :RIM], halo_ref.at[1], halo_send.at[1], halo_recv.at[1], r_down, col)

    def bias_slot(zb, xb, part=None):
        at = bias_ref.at[core, xb % 2, zb * 2 + xb // 2]
        return at if part is None else at.at[pl.ds(*part)]

    def bias_wait(role, zb, xb, part=None):
        wait(bias_slot(zb, xb, part), bias_send.at[role], bias_recv.at[role], row, col)

    def bias_give(role, zb, xb, peer, part=None):
        at = bias_slot(zb, xb, part)
        send(at, at, bias_send.at[role], bias_recv.at[role], row, peer)

    z_order = (zh, (zh + 3) % 4, (zh + 1) % 4, (zh + 2) % 4)

    def bias_z_own():
        bias_give(0, zh, x, z_up)
        bias_give(1, zh, x, z_down)

    def bias_z_pass():
        bias_wait(0, z_order[1], x)
        bias_give(2, z_order[1], x, z_up, PARTS[0])
        bias_wait(1, z_order[2], x)
        bias_give(3, z_order[2], x, z_down, PARTS[1])

    def bias_z_end():
        bias_wait(2, z_order[3], x, PARTS[0])
        bias_wait(3, z_order[3], x, PARTS[1])

    def bias_x_own(j):
        bias_give(4 + 4 * j, z_order[j], x, x_up)
        bias_give(5 + 4 * j, z_order[j], x, x_down)

    def bias_x_pass(j):
        bias_wait(4 + 4 * j, z_order[j], (x + 3) % 4)
        bias_give(6 + 4 * j, z_order[j], (x + 3) % 4, x_up, PARTS[0])
        bias_wait(5 + 4 * j, z_order[j], (x + 1) % 4)
        bias_give(7 + 4 * j, z_order[j], (x + 1) % 4, x_down, PARTS[1])

    def bias_x_end(j):
        bias_wait(6 + 4 * j, z_order[j], (x + 2) % 4, PARTS[0])
        bias_wait(7 + 4 * j, z_order[j], (x + 2) % 4, PARTS[1])
        at = bias_ref.at[core, :, pl.ds(z_order[j] * 2, 2)]
        send(at, at, twin_send.at[j], twin_recv.at[j], twin, col)

    def bias_end():
        for j in range(4):
            wait(bias_ref.at[1 - core, :, pl.ds(z_order[j] * 2, 2)], twin_send.at[j], twin_recv.at[j], twin, col)

    def tok_slot(late, yb, zb, part=None):
        at = tall_ref.at[core if late else 1 - core, yb * 2 + zb]
        return at if part is None else at.at[pl.ds(*part)]

    def tok_wait(late, role, yb, zb, part=None):
        n = late * 9 + role
        wait(tok_slot(late, yb, zb, part), tok_send.at[n], tok_recv.at[n], row, col)

    def tok_give(late, role, yb, zb, peer, part=None):
        at, n = tok_slot(late, yb, zb, part), late * 9 + role
        send(at, at, tok_send.at[n], tok_recv.at[n], peer, col)

    zs = (zl, 1 - zl)

    def tok_own(late):
        tok_give(late, 0, y, zl, zpair)
        tok_give(late, 1, y, zl, y_up)
        tok_give(late, 2, y, zl, y_down)

    def tok_second(late):
        tok_wait(late, 0, y, 1 - zl)
        tok_give(late, 5, y, 1 - zl, y_up)
        tok_give(late, 6, y, 1 - zl, y_down)

    def tok_pass(late, j):
        tok_wait(late, 1 + 4 * j, (y + 3) % 4, zs[j])
        tok_give(late, 3 + 4 * j, (y + 3) % 4, zs[j], y_up, PARTS[0])
        tok_wait(late, 2 + 4 * j, (y + 1) % 4, zs[j])
        tok_give(late, 4 + 4 * j, (y + 1) % 4, zs[j], y_down, PARTS[1])

    def tok_end(late):
        for j in range(2):
            tok_wait(late, 3 + 4 * j, (y + 2) % 4, zs[j], PARTS[0])
            tok_wait(late, 4 + 4 * j, (y + 2) % 4, zs[j], PARTS[1])

    pair_part(pair_ref, mask_ref, pair_w_ref, table_ref, bias_slot(zh, x), row, col)
    bias_z_own()
    bias_x_own(0)

    def windows(g):
        atom_windows(q_ref, k_ref, v_ref, att_ref, g * 12 * QWIN)

    def project(s):
        atom_project(s, halo_ref, feat_ref, wq[...], wk[...], wv[...], normed_ref, q_ref, k_ref, v_ref, row, rows)

    def tokens(s):
        return atom_tokens(s, feat_ref, token_ref, wo[...], agg_ref, gain_ref, att_ref, token_in_ref, row)

    wait(halo_ref.at[0], halo_send.at[0], halo_recv.at[0], r_up, col)
    wait(halo_ref.at[1], halo_send.at[1], halo_recv.at[1], r_down, col)
    project(1 - core)
    lax.fori_loop(0, 3, lambda g, c: (windows(g), c)[1], 0)
    give_ref[...] = tokens(1 - core)
    send(give_ref, tall_ref.at[core, y * 2 + zl], pass_send.at[0], pass_recv.at[0], twin, col)
    bias_x_pass(0)
    project(core)
    wait(tall_ref.at[1 - core, y * 2 + zl], pass_send.at[0], pass_recv.at[0], twin, col)
    tok_own(0)
    bias_z_pass()
    bias_x_own(1)
    bias_x_own(2)
    lax.fori_loop(0, 3, lambda g, c: (windows(g), c)[1], 0)
    tok_second(0)
    tok_pass(0, 0)
    bias_x_end(0)
    tall_ref[core, y * 2 + zl] = tokens(core)
    tok_own(1)
    tok_pass(0, 1)
    bias_z_end()
    bias_x_own(3)
    bias_x_pass(1)

    for load in loads:
        load.wait()
    wvt_ref[...] = weights_ref[2].astype(F32).T.astype(BF16)
    tok_second(1)
    tok_pass(1, 0)
    bias_x_pass(2)
    bias_x_end(1)
    for slab in range(2):
        block = tall_ref[core if slab else 1 - core, y * 2 + zl]
        qt_ref[slab] = dot(block, weights_ref[0])[:TOK].T.astype(BF16)
        sig_ref[slab] = jax.nn.sigmoid(dot(block, weights_ref[3])[:TOK])

    def project_tokens(which):
        base = pl.multiple_of(which * HALF, HALF)
        block = tall_ref[which].reshape(HALF, D)
        keys_ref[pl.ds(base, HALF), :] = dot(block, weights_ref[1]).astype(BF16)
        vt_ref[:, pl.ds(base, HALF)] = dot_nt(wvt_ref[...], block).astype(BF16)

    tok_end(0)
    project_tokens(1 - core)
    tok_pass(1, 1)
    bias_x_pass(3)
    bias_x_end(2)
    tok_end(1)
    project_tokens(core)
    bias_x_end(3)
    bias_end()

    def bias_of(slab, b, blk, lo, width):
        per = blk // PAD
        first = b * per
        at = bias_ref[core if slab else 1 - core, first // 8, first % 8 : first % 8 + per, :, lo : lo + width]
        return at.astype(F32).reshape(blk, width)

    def after_slab(slab):
        gated = mix_ref[slab] * sig_ref[slab]
        if slab == 0:
            back_send[...] = jnp.concatenate([gated, jnp.zeros((PAD - TOK, D), F32)], axis=0).astype(BF16)
            send(back_send, back_recv, pass_send.at[1], pass_recv.at[1], twin, col)
        else:
            out_ref[core] = (token_in_ref[core] + dot(gated.astype(BF16), weights_ref[4])).astype(BF16)

    attend(keys_ref, vt_ref, bias_of, qt_ref, scores_ref, p_ref, mix_ref, after_slab)
    wait(back_recv, pass_send.at[1], pass_recv.at[1], twin, col)
    out_ref[1 - core] = (token_in_ref[1 - core] + dot(back_recv[...], weights_ref[4])[:TOK]).astype(BF16)
    for copy in sent:
        copy.wait_send()


def shards(atom_feat, atom_token, pair_cond, token_mask, atom_wq, atom_wk, atom_wv, atom_wo, agg_weight, pair_weight,
           token_gain, query_weight, key_weight, value_weight, gate_weight, out_weight):
    whole = ATOMS + 2 * RIM
    dma = pltpu.SemaphoreType.DMA
    here, there = pl.BlockSpec(memory_space=pltpu.VMEM), pl.BlockSpec(memory_space=pl.ANY)
    return pl.pallas_call(
        whole_kernel,
        out_shape=jax.ShapeDtypeStruct((2, TOK, D), BF16),
        in_specs=[here] * 11 + [there] * 5,
        out_specs=here,
        scratch_shapes=[
            pltpu.VMEM((LANES, 128), F32), pltpu.VMEM((2, 2, RIM, CA), BF16), pltpu.VMEM((whole, CA), BF16),
            pltpu.VMEM((ATOMS, CA), BF16), pltpu.VMEM((whole, CA), BF16), pltpu.VMEM((whole, 2 * CA), BF16),
            pltpu.VMEM((ATOMS, CA), BF16), pltpu.VMEM((2, TOK, D), F32), pltpu.VMEM((PAD, D), BF16),
            pltpu.VMEM((2, 8, PAD, D), BF16), pltpu.VMEM((2, 2, 8, PAD, LANES), BF16), pltpu.VMEM((5, D, D), BF16),
            pltpu.VMEM((D, D), BF16), pltpu.VMEM((KEYS, D), BF16), pltpu.VMEM((D, KEYS), BF16),
            pltpu.VMEM((2, D, TOK), BF16), pltpu.VMEM((2, TOK, D), F32), pltpu.VMEM((2, KEYS, 256), F32),
            pltpu.VMEM((2, KEYS, 256), BF16), pltpu.VMEM((2, TOK, D), F32), pltpu.VMEM((PAD, D), BF16),
            pltpu.VMEM((PAD, D), BF16), dma((5,)), dma((2,)), dma((2,)), dma((20,)), dma((20,)), dma((4,)), dma((4,)),
            dma((18,)), dma((18,)), dma((2,)), dma((2,)),
        ],
        compiler_params=pltpu.CompilerParams(collective_id=0, has_side_effects=True, vmem_limit_bytes=60 * 1024 * 1024),
        name="whole",
    )(pair_cond, token_mask.reshape(1, TOK), pair_weight.T, atom_feat, atom_token.reshape(1, ATOMS), atom_wq, atom_wk,
      atom_wv, atom_wo, agg_weight, token_gain.reshape(1, D), query_weight, key_weight, value_weight, gate_weight, out_weight)


def solution(mesh):
    placed = (P("sample", "row", None), P("row"), P("row", "sample", None), P("sample")) + (P(),) * 12
    return jax.shard_map(shards, mesh=mesh, in_specs=placed, out_specs=P("sample", "row", None), check_vma=False)
```

```python
import jax
import jax.numpy as jnp
from jax import lax
from jax.experimental import pallas as pl
from jax.experimental.pallas import tpu as pltpu
from jax.sharding import PartitionSpec as P

HEADS = 16
HEAD_DIM = 48
AHEADS = 4
AHEAD_DIM = 32
QWIN = 32
KWIN = 128
RIM = 48
TOK = 72
PAD = 80
ATOMS = 1152
CA = 128
D = 768
LANES = HEADS * TOK
F32 = jnp.float32
BF16 = jnp.bfloat16
NEG = -1e30
CHUNKS = ((0, 256, 0, 256), (256, 256, 128, 256), (512, 256, 256, 384), (768, 128, 384, 256), (896, 256, 512, 256))


def dot(a, b):
    return jnp.dot(a, b, preferred_element_type=F32)


def dot_nt(a, b):
    return lax.dot_general(a, b, (((1,), (1,)), ((), ())), preferred_element_type=F32)


def layer_norm(x):
    mean = jnp.mean(x, -1, keepdims=True)
    centre = x - mean
    var = jnp.mean(centre * centre, -1, keepdims=True)
    return centre * lax.rsqrt(var + 1e-05)


def iota(shape, dim):
    return lax.broadcasted_iota(jnp.int32, shape, dim)


MESH = pl.DeviceIdType.MESH
KEYS = 16 * PAD
PAIR_ROWS = 12
HALF = 8 * PAD
GROUPS = ((0, 512), (512, 384), (896, 256))
WORK = ((1, 0), (1, 1), (0, 0), (0, 1), (1, 2), (1, 3), (0, 2), (0, 3), (0, 4), (1, 4))
PARTS = ((0, 48), (48, 32))


def pair_part(pair_load, pair_ref, mask_ref, weight_ref, table_ref, out, row, col, unroll=24):
    weight_t = weight_ref[...]

    def step(g, carry):
        for n in range(unroll // PAIR_ROWS):
            pair_load(g * (unroll // PAIR_ROWS) + n).wait()
        normed = [layer_norm(pair_ref[g * unroll + u].astype(F32)).astype(BF16) for u in range(unroll)]
        raw = [dot_nt(weight_t, n) for n in normed]
        for u in range(unroll):
            table_ref[pl.ds(g * unroll + u, HEADS, stride=TOK), :TOK] = raw[u]
        return carry

    lax.fori_loop(0, TOK // unroll, step, 0)
    kidx = col * TOK + iota((TOK, TOK), 1)
    qidx = row * TOK + iota((TOK, TOK), 0)
    allowed = (mask_ref[...][None, :] == 1) | (qidx == kidx)
    for h in range(HEADS):
        rows = pl.ds(h * TOK, TOK)
        table_ref[rows, :TOK] = jnp.where(allowed, table_ref[rows, :TOK], -30000.0)
    for n in range(LANES // 128):
        part = table_ref[n * 128 : (n + 1) * 128, :].T[:TOK]
        filled = jnp.concatenate([part, jnp.full((PAD - TOK, 128), NEG, F32)], axis=0)
        out[:, n * 128 : (n + 1) * 128] = filled.astype(BF16)


def atom_project(s, feat_ref, wq, wk, wv, q_ref, k_ref, v_ref):
    for c in range(3):
        normed = layer_norm(feat_ref[s, c * 384 : (c + 1) * 384].astype(F32)).astype(BF16)
        here = pl.ds(RIM + c * 384, 384)
        k_ref[s, here, :] = dot(normed, wk).astype(BF16)
        v_ref[s, here, :CA] = dot(normed, wv).astype(BF16)
        v_ref[s, here, CA:] = jnp.ones((384, CA), BF16)
        q_ref[s, pl.ds(c * 384, 384), :] = dot(normed, wq).astype(BF16)


def atom_rim(s, halo_ref, wk, wv, k_ref, v_ref, row, rows):
    last = RIM + ATOMS
    first_key = k_ref[s, RIM : RIM + 16, :].astype(F32)[:1]
    last_key = k_ref[s, last - 16 : last, :].astype(F32)[15:]
    for side, outside, start, key in ((0, row == 0, 0, first_key), (1, row == rows - 1, last, last_key)):
        normed = layer_norm(halo_ref[side, s].astype(F32)).astype(BF16)
        here = pl.ds(start, RIM)
        k_ref[s, here, :] = jnp.where(outside, jnp.broadcast_to(key, (RIM, CA)), dot(normed, wk)).astype(BF16)
        v_ref[s, here, :CA] = jnp.where(outside, 0.0, dot(normed, wv)).astype(BF16)
        v_ref[s, here, CA:] = jnp.where(outside, 0.0, jnp.ones((RIM, CA), F32)).astype(BF16)


def atom_windows(s, windows, q_ref, k_ref, v_ref, att_ref):
    head_of = iota((AHEADS * QWIN, CA), 0) // QWIN == iota((AHEADS * QWIN, CA), 1) // AHEAD_DIM
    lane_head = iota((QWIN, CA), 1) // AHEAD_DIM
    factor = 1.4426950408889634 / AHEAD_DIM**0.5
    starts = [w * QWIN for w in windows]
    scores = []
    for start in starts:
        q = q_ref[s, pl.ds(start, QWIN), :]
        stacked = jnp.where(head_of, jnp.concatenate([q] * AHEADS, axis=0), jnp.zeros((), BF16))
        scores.append(dot_nt(stacked, k_ref[s, pl.ds(start, KWIN), :]))
    exps = [jnp.exp2((sc - jnp.max(sc, -1, keepdims=True)) * factor).astype(BF16) for sc in scores]
    for start, e in zip(starts, exps):
        both = dot(e, v_ref[s, pl.ds(start, KWIN), :])
        top, low = both[:QWIN, :CA], both[:QWIN, CA:]
        for h in range(1, AHEADS):
            here = slice(h * QWIN, (h + 1) * QWIN)
            top = jnp.where(lane_head == h, both[here, :CA], top)
            low = jnp.where(lane_head == h, both[here, CA:], low)
        att_ref[s, pl.ds(start, QWIN), :] = (top / low).astype(BF16)


def atom_sum(s, chunks, feat_ref, token_ref, wo, agg_ref, att_ref, row):
    total = jnp.zeros((TOK, D), F32)
    for start, size in chunks:
        here = pl.ds(start, size)
        out = (feat_ref[s, here, :].astype(F32) + dot(att_ref[s, here, :], wo)).astype(BF16)
        hidden = jnp.maximum(dot(out, agg_ref[...]), 0.0).astype(BF16)
        onehot = token_ref[start : start + size][None, :] - row * TOK == iota((TOK, size), 0)
        total += dot(onehot.astype(BF16), hidden)
    return total


def token_counts(token_ref, row):
    onehot = token_ref[...][None, :] - row * TOK == iota((TOK, ATOMS), 0)
    return jnp.sum(onehot.astype(F32), -1, keepdims=True)


def token_norm(token_in, gain_ref):
    tnorm = layer_norm(token_in) * gain_ref[...][None, :]
    return jnp.concatenate([tnorm, jnp.zeros((PAD - TOK, D), F32)], axis=0).astype(BF16)


def query_prep(qt_ref, slab, chunk):
    lo, width, clo, cwidth = chunk
    lane = lo + iota((TOK, width), 1)
    fold = (lane % TOK == iota((TOK, width), 0)).astype(BF16)
    own_head = (lo + iota((cwidth, width), 1)) // TOK == (clo + iota((cwidth, width), 0)) // HEAD_DIM
    query = jnp.where(own_head, dot(qt_ref[slab, pl.ds(clo, cwidth), :], fold), 0.0).astype(BF16)
    return fold, own_head, query


def attend(k_ref, vt_ref, bias_of, qt_ref, scores_ref, p_ref, mix_ref, before, after_slab, blk=PAD * 2):
    mix_ref[...] = jnp.zeros_like(mix_ref)
    work = [(slab, CHUNKS[c]) for slab, c in WORK]
    blocks = KEYS // blk
    state = {}
    for i in range(len(work) + 2):
        before(i)
        now = work[i] if i < len(work) else None
        exps = work[i - 1] if 0 <= i - 1 < len(work) else None
        vals = work[i - 2] if i >= 2 else None
        if exps:
            top = jnp.max(state[i - 1][3], axis=0, keepdims=True)
            total = jnp.zeros((8, exps[1][1]), F32)
        if now:
            lo, width, clo, cwidth = now[1]
            state[i] = list(query_prep(qt_ref, *now)) + [jnp.full((8, width), -3e38, F32)]
            ahead = dot(k_ref[0:blk, clo : clo + cwidth], state[i][2])
        if vals:
            _, vwidth, vlo, vcwidth = vals[1]
            out = dot(vt_ref[pl.ds(vlo, vcwidth), :], p_ref[i % 2, :, :vwidth])
        for b in range(blocks):
            here = pl.ds(b * blk, blk)
            if now:
                raw = ahead
                if b + 1 < blocks:
                    ahead = dot(k_ref[(b + 1) * blk : (b + 2) * blk, clo : clo + cwidth], state[i][2])
            if exps:
                ewidth = exps[1][1]
                e = jnp.exp(scores_ref[(i - 1) % 2, here, :ewidth] - top)
                total += jnp.sum(e.reshape(blk // 8, 8, ewidth), axis=0)
                p_ref[(i - 1) % 2, here, :ewidth] = e.astype(BF16)
            if now:
                sc = raw * (1.0 / HEAD_DIM**0.5) + bias_of(now[0], b, blk, lo, width)
                scores_ref[i % 2, here, :width] = sc
                state[i][3] = jnp.maximum(state[i][3], jnp.max(sc.reshape(blk // 8, 8, width), axis=0))
        if exps:
            state[i - 1].append(jnp.sum(total, axis=0, keepdims=True))
        if vals:
            fold, own_head, _, _, vsum = state.pop(i - 2)
            out = jnp.where(own_head, out * (1.0 / vsum), 0.0)
            high = out.astype(BF16)
            rest = (out - high.astype(F32)).astype(BF16)
            mix_ref[vals[0], :, vlo : vlo + vcwidth] += dot_nt(fold, high) + dot_nt(fold, rest)
            if vals[1] == CHUNKS[-1]:
                after_slab(vals[0])


def whole_kernel(mask_ref, pair_w_ref, token_ref, wq, wk, wv, wo, gain_ref, pair_hbm, feat_hbm, agg_hbm,
                 query_hbm, key_hbm, value_hbm, gate_hbm, out_hbm, out_ref,
                 pair_ref, feat_ref, agg_ref, table_ref, halo_ref, q_ref, k_ref, v_ref, att_ref, token_in_ref, counts_ref, give_ref, tall_ref, bias_ref,
                 weights_ref, wvt_ref, keys_ref, vt_ref, qt_ref, sig_ref, scores_ref, p_ref, mix_ref, back_send, back_recv,
                 load_sem, halo_send, halo_recv, bias_send, bias_recv, twin_send, twin_recv, tok_send, tok_recv,
                 pass_send, pass_recv):
    row, col = lax.axis_index("row"), lax.axis_index("sample")
    rows, cols = lax.axis_size("row"), lax.axis_size("sample")
    core, zl, y = row % 2, (row // 2) % 2, row // 4
    x, zh = col % 4, col // 4
    twin, zpair = row + 1 - 2 * core, row + 2 - 4 * zl
    y_up, y_down = (row + 4) % rows, (row + rows - 4) % rows
    r_up, r_down = (row + 1) % rows, (row + rows - 1) % rows
    x_up, x_down = zh * 4 + (x + 1) % 4, zh * 4 + (x + 3) % 4
    z_up, z_down = (col + 4) % cols, (col + cols - 4) % cols
    def pair_load(n):
        here = pl.ds(n * PAIR_ROWS, PAIR_ROWS)
        return pltpu.make_async_copy(pair_hbm.at[here], pair_ref.at[here], load_sem.at[n])

    first = TOK // PAIR_ROWS
    for n in range(first):
        pair_load(n).start()
    sources = [(feat_hbm.at[0], feat_ref.at[0]), (feat_hbm.at[1], feat_ref.at[1]), (agg_hbm, agg_ref)]
    sources += [(source, weights_ref.at[n]) for n, source in enumerate((query_hbm, key_hbm, value_hbm, gate_hbm, out_hbm))]
    loads = [pltpu.make_async_copy(*pair, load_sem.at[first + n]) for n, pair in enumerate(sources)]
    for load in loads:
        load.start()

    barrier = pltpu.get_barrier_semaphore()
    for peer in (twin, zpair, y_up, y_down, r_up, r_down):
        pl.semaphore_signal(barrier, inc=1, device_id=(peer, col), device_id_type=MESH)
    for peer in (x_up, x_down, z_up, z_down):
        pl.semaphore_signal(barrier, inc=1, device_id=(row, peer), device_id_type=MESH)

    sent = []

    def send(src, dst, send_sem, recv_sem, peer_row, peer_col):
        copy = pltpu.make_async_remote_copy(src_ref=src, dst_ref=dst, send_sem=send_sem, recv_sem=recv_sem,
                                            device_id=(peer_row, peer_col), device_id_type=MESH)
        copy.start()
        sent.append(copy)

    def wait(dst, send_sem, recv_sem, peer_row, peer_col):
        pltpu.make_async_remote_copy(src_ref=dst, dst_ref=dst, send_sem=send_sem, recv_sem=recv_sem,
                                     device_id=(peer_row, peer_col), device_id_type=MESH).wait_recv()

    z_order = (zh, (zh + 3) % 4, (zh + 1) % 4, (zh + 2) % 4)

    def slot(g, zb, xb, part):
        rows_here = pl.ds(*part) if part else pl.ds(0, PAD)
        return bias_ref.at[core, xb % 2, zb, xb // 2, rows_here, pl.ds(*GROUPS[g])]

    def got(g, role, zb, xb, part=None):
        n = g * 20 + role
        wait(slot(g, zb, xb, part), bias_send.at[n], bias_recv.at[n], row, col)

    def give(g, role, zb, xb, peer, part=None):
        at, n = slot(g, zb, xb, part), g * 20 + role
        send(at, at, bias_send.at[n], bias_recv.at[n], row, peer)

    def z_own(g):
        give(g, 0, zh, x, z_up)
        give(g, 1, zh, x, z_down)

    def z_pass(g, way):
        got(g, way, z_order[1 + way], x)
        give(g, 2 + way, z_order[1 + way], x, z_down if way else z_up, PARTS[way])

    def z_end(g):
        got(g, 2, z_order[3], x, PARTS[0])
        got(g, 3, z_order[3], x, PARTS[1])

    def x_own(g, j):
        give(g, 4 + 4 * j, z_order[j], x, x_up)
        give(g, 5 + 4 * j, z_order[j], x, x_down)

    def x_pass(g, j, way):
        parts = PARTS if j % 2 else PARTS[::-1]
        origin = (x + 1) % 4 if way else (x + 3) % 4
        got(g, 4 + 4 * j + way, z_order[j], origin)
        give(g, 6 + 4 * j + way, z_order[j], origin, x_down if way else x_up, parts[way])

    def x_end(g, j):
        first, second = PARTS if j % 2 else PARTS[::-1]
        got(g, 6 + 4 * j, z_order[j], (x + 2) % 4, first)
        got(g, 7 + 4 * j, z_order[j], (x + 2) % 4, second)
        at, n = bias_ref.at[core, :, z_order[j], :, :, pl.ds(*GROUPS[g])], g * 4 + j
        send(at, at, twin_send.at[n], twin_recv.at[n], twin, col)

    def twin_end(g):
        for j in range(4):
            n = g * 4 + j
            at = bias_ref.at[1 - core, :, z_order[j], :, :, pl.ds(*GROUPS[g])]
            wait(at, twin_send.at[n], twin_recv.at[n], twin, col)

    def tok_slot(late, yb, zb, part=None):
        at = tall_ref.at[core if late else 1 - core, yb * 2 + zb]
        return at if part is None else at.at[pl.ds(*part)]

    def tok_wait(late, role, yb, zb, part=None):
        n = late * 9 + role
        wait(tok_slot(late, yb, zb, part), tok_send.at[n], tok_recv.at[n], row, col)

    def tok_give(late, role, yb, zb, peer, part=None):
        at, n = tok_slot(late, yb, zb, part), late * 9 + role
        send(at, at, tok_send.at[n], tok_recv.at[n], peer, col)

    zs = (zl, 1 - zl)

    def tok_own(late):
        tok_give(late, 0, y, zl, zpair)
        tok_give(late, 1, y, zl, y_up)
        tok_give(late, 2, y, zl, y_down)

    def tok_second(late):
        tok_wait(late, 0, y, 1 - zl)
        tok_give(late, 5, y, 1 - zl, y_up)
        tok_give(late, 6, y, 1 - zl, y_down)

    def tok_pass(late, j, way):
        origin = (y + 1) % 4 if way else (y + 3) % 4
        tok_wait(late, 1 + 4 * j + way, origin, zs[j])
        tok_give(late, 3 + 4 * j + way, origin, zs[j], y_down if way else y_up, PARTS[way])

    def tok_end(late):
        for j in range(2):
            tok_wait(late, 3 + 4 * j, (y + 2) % 4, zs[j], PARTS[0])
            tok_wait(late, 4 + 4 * j, (y + 2) % 4, zs[j], PARTS[1])

    def windows(s, which):
        atom_windows(s, which, q_ref, k_ref, v_ref, att_ref)

    def inner(s):
        token_in_ref[s] = atom_sum(s, ((128, 384), (512, 384), (896, 128)), feat_ref, token_ref, wo[...], agg_ref, att_ref,
                                   row)

    def tokens(s):
        edges = atom_sum(s, ((0, 128), (1024, 128)), feat_ref, token_ref, wo[...], agg_ref, att_ref, row)
        token_in = (token_in_ref[s] + edges) / counts_ref[:, :1]
        token_in_ref[s] = token_in
        return token_norm(token_in, gain_ref)

    def rim(s):
        atom_rim(s, halo_ref, wk[...], wv[...], k_ref, v_ref, row, rows)
        windows(s, (0, 1, ATOMS // QWIN - 2, ATOMS // QWIN - 1))

    pair_part(pair_load, pair_ref, mask_ref, pair_w_ref, table_ref, bias_ref.at[core, x % 2, zh, x // 2], row, col)
    loads[0].wait()
    loads[1].wait()
    for s in (1 - core, core):
        atom_project(s, feat_ref, wq[...], wk[...], wv[...], q_ref, k_ref, v_ref)
        for lo, hi in ((2, 14), (14, 26), (26, 34)):
            windows(s, range(lo, hi))

    pl.semaphore_wait(barrier, 10)
    send(feat_hbm.at[:, ATOMS - RIM :], halo_ref.at[0], halo_send.at[0], halo_recv.at[0], r_up, col)
    send(feat_hbm.at[:, :RIM], halo_ref.at[1], halo_send.at[1], halo_recv.at[1], r_down, col)

    def project_tokens(which):
        base = pl.multiple_of(which * HALF, HALF)
        block = tall_ref[which].reshape(HALF, D)
        keys_ref[pl.ds(base, HALF), :] = dot(block, weights_ref[1]).astype(BF16)
        vt_ref[:, pl.ds(base, HALF)] = dot_nt(wvt_ref[...], block).astype(BF16)

    z_own(0)
    x_own(0, 0)
    counts_ref[...] = jnp.broadcast_to(token_counts(token_ref, row), (TOK, 128))
    loads[2].wait()
    inner(1 - core)
    inner(core)
    for load in loads[3:]:
        load.wait()
    wvt_ref[...] = weights_ref[2].astype(F32).T.astype(BF16)
    x_own(1, 0)
    x_own(2, 0)
    z_own(1)
    wait(halo_ref.at[0], halo_send.at[0], halo_recv.at[0], r_up, col)
    wait(halo_ref.at[1], halo_send.at[1], halo_recv.at[1], r_down, col)
    rim(1 - core)
    give_ref[...] = tokens(1 - core)
    send(give_ref, tall_ref.at[core, y * 2 + zl], pass_send.at[0], pass_recv.at[0], twin, col)
    rim(core)
    tall_ref[core, y * 2 + zl] = tokens(core)
    tok_own(1)
    x_pass(0, 0, 0)
    x_pass(0, 0, 1)
    wait(tall_ref.at[1 - core, y * 2 + zl], pass_send.at[0], pass_recv.at[0], twin, col)
    tok_own(0)
    for slab in range(2):
        block = tall_ref[core if slab else 1 - core, y * 2 + zl]
        qt_ref[slab] = dot(block, weights_ref[0])[:TOK].T.astype(BF16)
        sig_ref[slab] = jax.nn.sigmoid(dot(block, weights_ref[3])[:TOK])
    x_pass(1, 0, 0)
    x_pass(1, 0, 1)
    x_pass(2, 0, 0)
    x_pass(2, 0, 1)
    z_pass(0, 0)
    x_own(0, 1)
    z_pass(0, 1)
    x_own(0, 2)
    x_end(0, 0)
    z_pass(1, 0)
    z_pass(1, 1)
    x_end(1, 0)
    x_own(1, 1)
    tok_pass(1, 0, 0)
    tok_pass(1, 0, 1)
    x_end(2, 0)
    tok_second(1)
    x_own(1, 2)
    x_pass(0, 1, 0)
    x_pass(0, 1, 1)
    tok_pass(0, 0, 0)
    tok_pass(0, 0, 1)
    x_pass(0, 2, 0)
    z_own(2)
    tok_second(0)
    x_pass(0, 2, 1)
    x_pass(1, 1, 0)
    x_pass(1, 1, 1)
    x_pass(1, 2, 0)
    tok_pass(1, 1, 1)
    x_pass(1, 2, 1)
    tok_pass(1, 1, 0)
    z_end(0)
    x_own(0, 3)
    x_end(0, 1)
    x_end(0, 2)
    z_end(1)
    x_own(1, 3)
    x_end(1, 1)
    z_pass(2, 1)
    x_own(2, 2)
    x_end(1, 2)
    tok_pass(0, 1, 1)
    z_pass(2, 0)
    x_own(2, 1)
    tok_pass(0, 1, 0)
    x_pass(0, 3, 0)
    x_pass(0, 3, 1)
    x_pass(1, 3, 0)
    x_pass(1, 3, 1)
    x_pass(2, 2, 0)
    x_pass(2, 2, 1)
    x_pass(2, 1, 0)
    x_pass(2, 1, 1)
    z_end(2)
    x_own(2, 3)
    tok_end(0)
    project_tokens(1 - core)
    x_end(0, 3)
    x_end(1, 3)
    x_end(2, 2)
    tok_end(1)
    project_tokens(core)
    x_pass(2, 3, 0)
    x_pass(2, 3, 1)
    x_end(2, 1)

    def before(i):
        if i == 2:
            twin_end(0)
        if i == 4:
            x_end(2, 3)
        if i == 6:
            twin_end(1)
        if i == 8:
            twin_end(2)

    def bias_of(slab, b, blk, lo, width):
        first = b * (blk // PAD)
        at = bias_ref[core if slab else 1 - core, first // 8, first % 8 // 2, :, :, lo : lo + width]
        return at.astype(F32).reshape(blk, width)

    def after_slab(slab):
        gated = mix_ref[slab] * sig_ref[slab]
        if slab == 0:
            back_send[...] = jnp.concatenate([gated, jnp.zeros((PAD - TOK, D), F32)], axis=0).astype(BF16)
            send(back_send, back_recv, pass_send.at[1], pass_recv.at[1], twin, col)
        else:
            out_ref[core] = (token_in_ref[core] + dot(gated.astype(BF16), weights_ref[4])).astype(BF16)

    attend(keys_ref, vt_ref, bias_of, qt_ref, scores_ref, p_ref, mix_ref, before, after_slab)
    wait(back_recv, pass_send.at[1], pass_recv.at[1], twin, col)
    out_ref[1 - core] = (token_in_ref[1 - core] + dot(back_recv[...], weights_ref[4])[:TOK]).astype(BF16)
    for copy in sent:
        copy.wait_send()


def shards(atom_feat, atom_token, pair_cond, token_mask, atom_wq, atom_wk, atom_wv, atom_wo, agg_weight, pair_weight,
           token_gain, query_weight, key_weight, value_weight, gate_weight, out_weight):
    whole = ATOMS + 2 * RIM
    dma = pltpu.SemaphoreType.DMA
    here, there = pl.BlockSpec(memory_space=pltpu.VMEM), pl.BlockSpec(memory_space=pl.ANY)
    return pl.pallas_call(
        whole_kernel,
        out_shape=jax.ShapeDtypeStruct((2, TOK, D), BF16),
        in_specs=[here] * 8 + [there] * 8,
        out_specs=here,
        scratch_shapes=[
            pltpu.VMEM((TOK, TOK, 128), BF16), pltpu.VMEM((2, ATOMS, CA), BF16), pltpu.VMEM((CA, D), BF16),
            pltpu.VMEM((LANES, 128), F32), pltpu.VMEM((2, 2, RIM, CA), BF16),
            pltpu.VMEM((2, ATOMS, CA), BF16), pltpu.VMEM((2, whole, CA), BF16), pltpu.VMEM((2, whole, 2 * CA), BF16),
            pltpu.VMEM((2, ATOMS, CA), BF16), pltpu.VMEM((2, TOK, D), F32), pltpu.VMEM((TOK, 128), F32), pltpu.VMEM((PAD, D), BF16),
            pltpu.VMEM((2, 8, PAD, D), BF16), pltpu.VMEM((2, 2, 4, 2, PAD, LANES), BF16), pltpu.VMEM((5, D, D), BF16),
            pltpu.VMEM((D, D), BF16), pltpu.VMEM((KEYS, D), BF16), pltpu.VMEM((D, KEYS), BF16),
            pltpu.VMEM((2, D, TOK), BF16), pltpu.VMEM((2, TOK, D), F32), pltpu.VMEM((2, KEYS, 256), F32),
            pltpu.VMEM((2, KEYS, 256), BF16), pltpu.VMEM((2, TOK, D), F32), pltpu.VMEM((PAD, D), BF16),
            pltpu.VMEM((PAD, D), BF16), dma((14,)), dma((2,)), dma((2,)), dma((60,)), dma((60,)), dma((12,)), dma((12,)),
            dma((18,)), dma((18,)), dma((2,)), dma((2,)),
        ],
        compiler_params=pltpu.CompilerParams(collective_id=0, has_side_effects=True, vmem_limit_bytes=60 * 1024 * 1024),
        name="whole",
    )(token_mask, pair_weight.T, atom_token, atom_wq, atom_wk, atom_wv, atom_wo, token_gain, pair_cond, atom_feat,
      agg_weight, query_weight, key_weight, value_weight, gate_weight, out_weight)


def solution(mesh):
    placed = (P("sample", "row", None), P("row"), P("row", "sample", None), P("sample")) + (P(),) * 12
    return jax.shard_map(shards, mesh=mesh, in_specs=placed, out_specs=P("sample", "row", None), check_vma=False)
```

```python
import jax
import jax.numpy as jnp
from jax import lax
from jax.experimental import pallas as pl
from jax.experimental.pallas import tpu as pltpu
from jax.sharding import PartitionSpec as P

HEADS = 16
HEAD_DIM = 48
AHEADS = 4
AHEAD_DIM = 32
QWIN = 32
KWIN = 128
RIM = 48
TOK = 72
PAD = 80
ATOMS = 1152
CA = 128
D = 768
LANES = HEADS * TOK
F32 = jnp.float32
BF16 = jnp.bfloat16
NEG = -1e30
CHUNKS = ((0, 256, 0, 256), (256, 256, 128, 256), (512, 256, 256, 384), (768, 128, 384, 256), (896, 256, 512, 256))


def dot(a, b):
    return jnp.dot(a, b, preferred_element_type=F32)


def dot_nt(a, b):
    return lax.dot_general(a, b, (((1,), (1,)), ((), ())), preferred_element_type=F32)


def layer_norm(x):
    mean = jnp.mean(x, -1, keepdims=True)
    centre = x - mean
    var = jnp.mean(centre * centre, -1, keepdims=True)
    return centre * lax.rsqrt(var + 1e-05)


def iota(shape, dim):
    return lax.broadcasted_iota(jnp.int32, shape, dim)


MESH = pl.DeviceIdType.MESH
KEYS = 16 * PAD
PAIR_ROWS = 12
HALF = 8 * PAD
GROUPS = ((0, 256), (256, 512), (768, 384))
WORK = ((1, 0), (0, 0), (1, 1), (1, 2), (0, 1), (0, 2), (1, 3), (0, 3), (0, 4), (1, 4))
PARTS = ((0, 48), (48, 32))


def pair_part(pair_load, pair_ref, mask_ref, weight_ref, table_ref, out, row, col, unroll=24):
    weight_t = weight_ref[...]

    def step(g, carry):
        for n in range(unroll // PAIR_ROWS):
            pair_load(g * (unroll // PAIR_ROWS) + n).wait()
        normed = [layer_norm(pair_ref[g * unroll + u].astype(F32)).astype(BF16) for u in range(unroll)]
        raw = [dot_nt(weight_t, n) for n in normed]
        for u in range(unroll):
            table_ref[pl.ds(g * unroll + u, HEADS, stride=TOK), :TOK] = raw[u]
        return carry

    lax.fori_loop(0, TOK // unroll, step, 0)
    kidx = col * TOK + iota((TOK, TOK), 1)
    qidx = row * TOK + iota((TOK, TOK), 0)
    allowed = (mask_ref[...][None, :] == 1) | (qidx == kidx)
    for h in range(HEADS):
        rows = pl.ds(h * TOK, TOK)
        table_ref[rows, :TOK] = jnp.where(allowed, table_ref[rows, :TOK], -30000.0)
    for n in range(LANES // 128):
        part = table_ref[n * 128 : (n + 1) * 128, :].T[:TOK]
        filled = jnp.concatenate([part, jnp.full((PAD - TOK, 128), NEG, F32)], axis=0)
        out[:, n * 128 : (n + 1) * 128] = filled.astype(BF16)


def atom_project(s, feat_ref, wq, wk, wv, q_ref, k_ref, v_ref):
    for c in range(3):
        normed = layer_norm(feat_ref[s, c * 384 : (c + 1) * 384].astype(F32)).astype(BF16)
        here = pl.ds(RIM + c * 384, 384)
        k_ref[s, here, :] = dot(normed, wk).astype(BF16)
        v_ref[s, here, :CA] = dot(normed, wv).astype(BF16)
        v_ref[s, here, CA:] = jnp.ones((384, CA), BF16)
        q_ref[s, pl.ds(c * 384, 384), :] = dot(normed, wq).astype(BF16)


def atom_rim(s, halo_ref, wk, wv, k_ref, v_ref, row, rows):
    last = RIM + ATOMS
    first_key = k_ref[s, RIM : RIM + 16, :].astype(F32)[:1]
    last_key = k_ref[s, last - 16 : last, :].astype(F32)[15:]
    for side, outside, start, key in ((0, row == 0, 0, first_key), (1, row == rows - 1, last, last_key)):
        normed = layer_norm(halo_ref[side, s].astype(F32)).astype(BF16)
        here = pl.ds(start, RIM)
        k_ref[s, here, :] = jnp.where(outside, jnp.broadcast_to(key, (RIM, CA)), dot(normed, wk)).astype(BF16)
        v_ref[s, here, :CA] = jnp.where(outside, 0.0, dot(normed, wv)).astype(BF16)
        v_ref[s, here, CA:] = jnp.where(outside, 0.0, jnp.ones((RIM, CA), F32)).astype(BF16)


def atom_windows(s, windows, q_ref, k_ref, v_ref, att_ref):
    head_of = iota((AHEADS * QWIN, CA), 0) // QWIN == iota((AHEADS * QWIN, CA), 1) // AHEAD_DIM
    lane_head = iota((QWIN, CA), 1) // AHEAD_DIM
    factor = 1.4426950408889634 / AHEAD_DIM**0.5
    starts = [w * QWIN for w in windows]
    scores = []
    for start in starts:
        q = q_ref[s, pl.ds(start, QWIN), :]
        stacked = jnp.where(head_of, jnp.concatenate([q] * AHEADS, axis=0), jnp.zeros((), BF16))
        scores.append(dot_nt(stacked, k_ref[s, pl.ds(start, KWIN), :]))
    exps = [jnp.exp2((sc - jnp.max(sc, -1, keepdims=True)) * factor).astype(BF16) for sc in scores]
    for start, e in zip(starts, exps):
        both = dot(e, v_ref[s, pl.ds(start, KWIN), :])
        top, low = both[:QWIN, :CA], both[:QWIN, CA:]
        for h in range(1, AHEADS):
            here = slice(h * QWIN, (h + 1) * QWIN)
            top = jnp.where(lane_head == h, both[here, :CA], top)
            low = jnp.where(lane_head == h, both[here, CA:], low)
        att_ref[s, pl.ds(start, QWIN), :] = (top / low).astype(BF16)


def atom_sum(s, chunks, feat_ref, token_ref, wo, agg_ref, att_ref, row):
    total = jnp.zeros((TOK, D), F32)
    for start, size in chunks:
        here = pl.ds(start, size)
        out = (feat_ref[s, here, :].astype(F32) + dot(att_ref[s, here, :], wo)).astype(BF16)
        hidden = jnp.maximum(dot(out, agg_ref[...]), 0.0).astype(BF16)
        onehot = token_ref[start : start + size][None, :] - row * TOK == iota((TOK, size), 0)
        total += dot(onehot.astype(BF16), hidden)
    return total


def token_counts(token_ref, row):
    onehot = token_ref[...][None, :] - row * TOK == iota((TOK, ATOMS), 0)
    return jnp.sum(onehot.astype(F32), -1, keepdims=True)


def token_norm(token_in, gain_ref):
    tnorm = layer_norm(token_in) * gain_ref[...][None, :]
    return jnp.concatenate([tnorm, jnp.zeros((PAD - TOK, D), F32)], axis=0).astype(BF16)


def query_prep(qt_ref, slab, chunk):
    lo, width, clo, cwidth = chunk
    lane = lo + iota((TOK, width), 1)
    fold = (lane % TOK == iota((TOK, width), 0)).astype(BF16)
    own_head = (lo + iota((cwidth, width), 1)) // TOK == (clo + iota((cwidth, width), 0)) // HEAD_DIM
    query = jnp.where(own_head, dot(qt_ref[slab, pl.ds(clo, cwidth), :], fold), 0.0).astype(BF16)
    return fold, own_head, query


def attend(k_ref, vt_ref, bias_of, qt_ref, scores_ref, p_ref, mix_ref, before, after_slab, blk=PAD * 2):
    mix_ref[...] = jnp.zeros_like(mix_ref)
    work = [(slab, CHUNKS[c]) for slab, c in WORK]
    blocks = KEYS // blk
    state = {}
    for i in range(len(work) + 2):
        before(i)
        now = work[i] if i < len(work) else None
        exps = work[i - 1] if 0 <= i - 1 < len(work) else None
        vals = work[i - 2] if i >= 2 else None
        if exps:
            top = jnp.max(state[i - 1][3], axis=0, keepdims=True)
            total = jnp.zeros((8, exps[1][1]), F32)
        if now:
            lo, width, clo, cwidth = now[1]
            state[i] = list(query_prep(qt_ref, *now)) + [jnp.full((8, width), -3e38, F32)]
            ahead = dot(k_ref[0:blk, clo : clo + cwidth], state[i][2])
        if vals:
            _, vwidth, vlo, vcwidth = vals[1]
            out = dot(vt_ref[pl.ds(vlo, vcwidth), :], p_ref[i % 2, :, :vwidth])
        for b in range(blocks):
            here = pl.ds(b * blk, blk)
            if now:
                raw = ahead
                if b + 1 < blocks:
                    ahead = dot(k_ref[(b + 1) * blk : (b + 2) * blk, clo : clo + cwidth], state[i][2])
            if exps:
                ewidth = exps[1][1]
                e = jnp.exp(scores_ref[(i - 1) % 2, here, :ewidth] - top)
                total += jnp.sum(e.reshape(blk // 8, 8, ewidth), axis=0)
                p_ref[(i - 1) % 2, here, :ewidth] = e.astype(BF16)
            if now:
                sc = raw * (1.0 / HEAD_DIM**0.5) + bias_of(now[0], b, blk, lo, width)
                scores_ref[i % 2, here, :width] = sc
                state[i][3] = jnp.maximum(state[i][3], jnp.max(sc.reshape(blk // 8, 8, width), axis=0))
        if exps:
            state[i - 1].append(jnp.sum(total, axis=0, keepdims=True))
        if vals:
            fold, own_head, _, _, vsum = state.pop(i - 2)
            out = jnp.where(own_head, out * (1.0 / vsum), 0.0)
            high = out.astype(BF16)
            rest = (out - high.astype(F32)).astype(BF16)
            mix_ref[vals[0], :, vlo : vlo + vcwidth] += dot_nt(fold, high) + dot_nt(fold, rest)
            if vals[1] == CHUNKS[-1]:
                after_slab(vals[0])


def whole_kernel(mask_ref, pair_w_ref, token_ref, wq, wk, wv, wo, gain_ref, pair_hbm, feat_hbm, agg_hbm,
                 query_hbm, key_hbm, value_hbm, gate_hbm, out_hbm, out_ref,
                 pair_ref, feat_ref, agg_ref, table_ref, halo_ref, q_ref, k_ref, v_ref, att_ref, token_in_ref, counts_ref, give_ref, tall_ref, bias_ref,
                 weights_ref, wvt_ref, keys_ref, vt_ref, qt_ref, sig_ref, scores_ref, p_ref, mix_ref, back_send, back_recv,
                 load_sem, halo_send, halo_recv, bias_send, bias_recv, twin_send, twin_recv, tok_send, tok_recv,
                 pass_send, pass_recv):
    row, col = lax.axis_index("row"), lax.axis_index("sample")
    rows, cols = lax.axis_size("row"), lax.axis_size("sample")
    core, zl, y = row % 2, (row // 2) % 2, row // 4
    x, zh = col % 4, col // 4
    twin, zpair = row + 1 - 2 * core, row + 2 - 4 * zl
    y_up, y_down = (row + 4) % rows, (row + rows - 4) % rows
    r_up, r_down = (row + 1) % rows, (row + rows - 1) % rows
    x_up, x_down = zh * 4 + (x + 1) % 4, zh * 4 + (x + 3) % 4
    z_up, z_down = (col + 4) % cols, (col + cols - 4) % cols
    def pair_load(n):
        here = pl.ds(n * PAIR_ROWS, PAIR_ROWS)
        return pltpu.make_async_copy(pair_hbm.at[here], pair_ref.at[here], load_sem.at[n])

    first = TOK // PAIR_ROWS
    for n in range(first):
        pair_load(n).start()
    sources = [(feat_hbm.at[0], feat_ref.at[0]), (feat_hbm.at[1], feat_ref.at[1]), (agg_hbm, agg_ref)]
    sources += [(source, weights_ref.at[n]) for n, source in enumerate((query_hbm, key_hbm, value_hbm, gate_hbm, out_hbm))]
    loads = [pltpu.make_async_copy(*pair, load_sem.at[first + n]) for n, pair in enumerate(sources)]
    for load in loads:
        load.start()

    barrier = pltpu.get_barrier_semaphore()
    for peer in (twin, zpair, y_up, y_down, r_up, r_down):
        pl.semaphore_signal(barrier, inc=1, device_id=(peer, col), device_id_type=MESH)
    for peer in (x_up, x_down, z_up, z_down):
        pl.semaphore_signal(barrier, inc=1, device_id=(row, peer), device_id_type=MESH)

    sent = []

    def send(src, dst, send_sem, recv_sem, peer_row, peer_col):
        copy = pltpu.make_async_remote_copy(src_ref=src, dst_ref=dst, send_sem=send_sem, recv_sem=recv_sem,
                                            device_id=(peer_row, peer_col), device_id_type=MESH)
        copy.start()
        sent.append(copy)

    def wait(dst, send_sem, recv_sem, peer_row, peer_col):
        pltpu.make_async_remote_copy(src_ref=dst, dst_ref=dst, send_sem=send_sem, recv_sem=recv_sem,
                                     device_id=(peer_row, peer_col), device_id_type=MESH).wait_recv()

    z_order = (zh, (zh + 3) % 4, (zh + 1) % 4, (zh + 2) % 4)

    def slot(g, zb, xb, part):
        rows_here = pl.ds(*part) if part else pl.ds(0, PAD)
        return bias_ref.at[core, xb % 2, zb, xb // 2, rows_here, pl.ds(*GROUPS[g])]

    def got(g, role, zb, xb, part=None):
        n = g * 20 + role
        wait(slot(g, zb, xb, part), bias_send.at[n], bias_recv.at[n], row, col)

    def give(g, role, zb, xb, peer, part=None):
        at, n = slot(g, zb, xb, part), g * 20 + role
        send(at, at, bias_send.at[n], bias_recv.at[n], row, peer)

    def z_own(g):
        give(g, 0, zh, x, z_up)
        give(g, 1, zh, x, z_down)

    def z_pass(g, way):
        got(g, way, z_order[1 + way], x)
        give(g, 2 + way, z_order[1 + way], x, z_down if way else z_up, PARTS[way])

    def z_end(g):
        got(g, 2, z_order[3], x, PARTS[0])
        got(g, 3, z_order[3], x, PARTS[1])

    def x_own(g, j):
        give(g, 4 + 4 * j, z_order[j], x, x_up)
        give(g, 5 + 4 * j, z_order[j], x, x_down)

    def x_pass(g, j, way):
        parts = PARTS if j % 2 else PARTS[::-1]
        origin = (x + 1) % 4 if way else (x + 3) % 4
        got(g, 4 + 4 * j + way, z_order[j], origin)
        give(g, 6 + 4 * j + way, z_order[j], origin, x_down if way else x_up, parts[way])

    def x_end(g, j):
        first, second = PARTS if j % 2 else PARTS[::-1]
        got(g, 6 + 4 * j, z_order[j], (x + 2) % 4, first)
        got(g, 7 + 4 * j, z_order[j], (x + 2) % 4, second)
        at, n = bias_ref.at[core, :, z_order[j], :, :, pl.ds(*GROUPS[g])], g * 4 + j
        send(at, at, twin_send.at[n], twin_recv.at[n], twin, col)

    def twin_end(g):
        for j in range(4):
            n = g * 4 + j
            at = bias_ref.at[1 - core, :, z_order[j], :, :, pl.ds(*GROUPS[g])]
            wait(at, twin_send.at[n], twin_recv.at[n], twin, col)

    def tok_slot(late, yb, zb, part=None):
        at = tall_ref.at[core if late else 1 - core, yb * 2 + zb]
        return at if part is None else at.at[pl.ds(*part)]

    def tok_wait(late, role, yb, zb, part=None):
        n = late * 9 + role
        wait(tok_slot(late, yb, zb, part), tok_send.at[n], tok_recv.at[n], row, col)

    def tok_give(late, role, yb, zb, peer, part=None):
        at, n = tok_slot(late, yb, zb, part), late * 9 + role
        send(at, at, tok_send.at[n], tok_recv.at[n], peer, col)

    zs = (zl, 1 - zl)

    def tok_own(late):
        tok_give(late, 0, y, zl, zpair)
        tok_give(late, 1, y, zl, y_up)
        tok_give(late, 2, y, zl, y_down)

    def tok_second(late):
        tok_wait(late, 0, y, 1 - zl)
        tok_give(late, 5, y, 1 - zl, y_up)
        tok_give(late, 6, y, 1 - zl, y_down)

    def tok_pass(late, j, way):
        origin = (y + 1) % 4 if way else (y + 3) % 4
        tok_wait(late, 1 + 4 * j + way, origin, zs[j])
        tok_give(late, 3 + 4 * j + way, origin, zs[j], y_down if way else y_up, PARTS[way])

    def tok_end(late):
        for j in range(2):
            tok_wait(late, 3 + 4 * j, (y + 2) % 4, zs[j], PARTS[0])
            tok_wait(late, 4 + 4 * j, (y + 2) % 4, zs[j], PARTS[1])

    def windows(s, which):
        atom_windows(s, which, q_ref, k_ref, v_ref, att_ref)

    def inner(s):
        token_in_ref[s] = atom_sum(s, ((128, 384), (512, 384), (896, 128)), feat_ref, token_ref, wo[...], agg_ref, att_ref,
                                   row)

    def tokens(s):
        edges = atom_sum(s, ((0, 128), (1024, 128)), feat_ref, token_ref, wo[...], agg_ref, att_ref, row)
        token_in = (token_in_ref[s] + edges) / counts_ref[:, :1]
        token_in_ref[s] = token_in
        return token_norm(token_in, gain_ref)

    def rim(s):
        atom_rim(s, halo_ref, wk[...], wv[...], k_ref, v_ref, row, rows)
        windows(s, (0, 1, ATOMS // QWIN - 2, ATOMS // QWIN - 1))

    pair_part(pair_load, pair_ref, mask_ref, pair_w_ref, table_ref, bias_ref.at[core, x % 2, zh, x // 2], row, col)
    loads[0].wait()
    loads[1].wait()
    for s in (1 - core, core):
        atom_project(s, feat_ref, wq[...], wk[...], wv[...], q_ref, k_ref, v_ref)
        for lo, hi in ((2, 14), (14, 26), (26, 34)):
            windows(s, range(lo, hi))

    pl.semaphore_wait(barrier, 10)
    send(feat_hbm.at[:, ATOMS - RIM :], halo_ref.at[0], halo_send.at[0], halo_recv.at[0], r_up, col)
    send(feat_hbm.at[:, :RIM], halo_ref.at[1], halo_send.at[1], halo_recv.at[1], r_down, col)

    def project_tokens(which):
        base = pl.multiple_of(which * HALF, HALF)
        block = tall_ref[which].reshape(HALF, D)
        keys_ref[pl.ds(base, HALF), :] = dot(block, weights_ref[1]).astype(BF16)
        vt_ref[:, pl.ds(base, HALF)] = dot_nt(wvt_ref[...], block).astype(BF16)

    z_own(0)
    x_own(0, 0)
    counts_ref[...] = jnp.broadcast_to(token_counts(token_ref, row), (TOK, 128))
    loads[2].wait()
    inner(1 - core)
    z_own(1)
    x_own(1, 0)
    inner(core)
    for load in loads[3:]:
        load.wait()
    wvt_ref[...] = weights_ref[2].astype(F32).T.astype(BF16)
    x_own(2, 0)
    wait(halo_ref.at[0], halo_send.at[0], halo_recv.at[0], r_up, col)
    wait(halo_ref.at[1], halo_send.at[1], halo_recv.at[1], r_down, col)
    rim(1 - core)
    x_pass(0, 0, 0)
    x_pass(0, 0, 1)
    give_ref[...] = tokens(1 - core)
    send(give_ref, tall_ref.at[core, y * 2 + zl], pass_send.at[0], pass_recv.at[0], twin, col)
    rim(core)
    tall_ref[core, y * 2 + zl] = tokens(core)
    tok_own(1)
    z_pass(0, 0)
    z_pass(0, 1)
    wait(tall_ref.at[1 - core, y * 2 + zl], pass_send.at[0], pass_recv.at[0], twin, col)
    tok_own(0)
    x_own(0, 1)
    for slab in range(2):
        block = tall_ref[core if slab else 1 - core, y * 2 + zl]
        qt_ref[slab] = dot(block, weights_ref[0])[:TOK].T.astype(BF16)
        sig_ref[slab] = jax.nn.sigmoid(dot(block, weights_ref[3])[:TOK])
    x_own(0, 2)
    x_pass(1, 0, 0)
    x_pass(1, 0, 1)
    x_pass(2, 0, 0)
    x_pass(2, 0, 1)
    x_end(0, 0)
    z_pass(1, 0)
    z_pass(1, 1)
    x_pass(0, 1, 0)
    x_pass(0, 1, 1)
    x_own(1, 1)
    tok_pass(1, 0, 0)
    tok_pass(1, 0, 1)
    tok_second(1)
    x_pass(0, 2, 0)
    x_pass(0, 2, 1)
    x_end(1, 0)
    x_own(1, 2)
    x_end(2, 0)
    x_end(0, 1)
    tok_pass(0, 0, 0)
    tok_pass(0, 0, 1)
    z_own(2)
    z_end(0)
    x_own(0, 3)
    tok_second(0)
    x_pass(1, 1, 0)
    x_pass(1, 1, 1)
    x_end(0, 2)
    tok_pass(1, 1, 1)
    x_pass(1, 2, 0)
    tok_pass(1, 1, 0)
    x_pass(1, 2, 1)
    x_pass(0, 3, 0)
    z_end(1)
    x_own(1, 3)
    x_pass(0, 3, 1)
    x_end(1, 1)
    z_pass(2, 1)
    z_pass(2, 0)
    x_own(2, 1)
    tok_pass(0, 1, 1)
    x_end(1, 2)
    tok_pass(0, 1, 0)
    x_own(2, 2)
    x_pass(1, 3, 0)
    x_pass(1, 3, 1)
    x_end(0, 3)
    x_pass(2, 1, 0)
    x_pass(2, 1, 1)
    z_end(2)
    x_own(2, 3)
    tok_end(0)
    project_tokens(1 - core)
    x_end(1, 3)
    x_pass(2, 2, 0)
    x_pass(2, 2, 1)
    tok_end(1)
    project_tokens(core)
    x_end(2, 1)
    x_pass(2, 3, 0)
    x_pass(2, 3, 1)

    def before(i):
        if i == 1:
            twin_end(0)
        if i == 2:
            x_end(2, 2)
        if i == 4:
            x_end(2, 3)
            twin_end(1)
        if i == 7:
            twin_end(2)

    def bias_of(slab, b, blk, lo, width):
        first = b * (blk // PAD)
        at = bias_ref[core if slab else 1 - core, first // 8, first % 8 // 2, :, :, lo : lo + width]
        return at.astype(F32).reshape(blk, width)

    def after_slab(slab):
        gated = mix_ref[slab] * sig_ref[slab]
        if slab == 0:
            back_send[...] = jnp.concatenate([gated, jnp.zeros((PAD - TOK, D), F32)], axis=0).astype(BF16)
            send(back_send, back_recv, pass_send.at[1], pass_recv.at[1], twin, col)
        else:
            out_ref[core] = (token_in_ref[core] + dot(gated.astype(BF16), weights_ref[4])).astype(BF16)

    attend(keys_ref, vt_ref, bias_of, qt_ref, scores_ref, p_ref, mix_ref, before, after_slab)
    wait(back_recv, pass_send.at[1], pass_recv.at[1], twin, col)
    out_ref[1 - core] = (token_in_ref[1 - core] + dot(back_recv[...], weights_ref[4])[:TOK]).astype(BF16)
    for copy in sent:
        copy.wait_send()


def shards(atom_feat, atom_token, pair_cond, token_mask, atom_wq, atom_wk, atom_wv, atom_wo, agg_weight, pair_weight,
           token_gain, query_weight, key_weight, value_weight, gate_weight, out_weight):
    whole = ATOMS + 2 * RIM
    dma = pltpu.SemaphoreType.DMA
    here, there = pl.BlockSpec(memory_space=pltpu.VMEM), pl.BlockSpec(memory_space=pl.ANY)
    return pl.pallas_call(
        whole_kernel,
        out_shape=jax.ShapeDtypeStruct((2, TOK, D), BF16),
        in_specs=[here] * 8 + [there] * 8,
        out_specs=here,
        scratch_shapes=[
            pltpu.VMEM((TOK, TOK, 128), BF16), pltpu.VMEM((2, ATOMS, CA), BF16), pltpu.VMEM((CA, D), BF16),
            pltpu.VMEM((LANES, 128), F32), pltpu.VMEM((2, 2, RIM, CA), BF16),
            pltpu.VMEM((2, ATOMS, CA), BF16), pltpu.VMEM((2, whole, CA), BF16), pltpu.VMEM((2, whole, 2 * CA), BF16),
            pltpu.VMEM((2, ATOMS, CA), BF16), pltpu.VMEM((2, TOK, D), F32), pltpu.VMEM((TOK, 128), F32), pltpu.VMEM((PAD, D), BF16),
            pltpu.VMEM((2, 8, PAD, D), BF16), pltpu.VMEM((2, 2, 4, 2, PAD, LANES), BF16), pltpu.VMEM((5, D, D), BF16),
            pltpu.VMEM((D, D), BF16), pltpu.VMEM((KEYS, D), BF16), pltpu.VMEM((D, KEYS), BF16),
            pltpu.VMEM((2, D, TOK), BF16), pltpu.VMEM((2, TOK, D), F32), pltpu.VMEM((2, KEYS, 256), F32),
            pltpu.VMEM((2, KEYS, 256), BF16), pltpu.VMEM((2, TOK, D), F32), pltpu.VMEM((PAD, D), BF16),
            pltpu.VMEM((PAD, D), BF16), dma((14,)), dma((2,)), dma((2,)), dma((60,)), dma((60,)), dma((12,)), dma((12,)),
            dma((18,)), dma((18,)), dma((2,)), dma((2,)),
        ],
        compiler_params=pltpu.CompilerParams(collective_id=0, has_side_effects=True, vmem_limit_bytes=60 * 1024 * 1024),
        name="whole",
    )(token_mask, pair_weight.T, atom_token, atom_wq, atom_wk, atom_wv, atom_wo, token_gain, pair_cond, atom_feat,
      agg_weight, query_weight, key_weight, value_weight, gate_weight, out_weight)


def solution(mesh):
    placed = (P("sample", "row", None), P("row"), P("row", "sample", None), P("sample")) + (P(),) * 12
    return jax.shard_map(shards, mesh=mesh, in_specs=placed, out_specs=P("sample", "row", None), check_vma=False)
```

```python
import jax
import jax.numpy as jnp
from jax import lax
from jax.experimental import pallas as pl
from jax.experimental.pallas import tpu as pltpu
from jax.sharding import PartitionSpec as P

HEADS = 16
HEAD_DIM = 48
AHEADS = 4
AHEAD_DIM = 32
QWIN = 32
KWIN = 128
RIM = 48
TOK = 72
PAD = 80
ATOMS = 1152
CA = 128
D = 768
LANES = HEADS * TOK
F32 = jnp.float32
BF16 = jnp.bfloat16
NEG = -1e30
CHUNKS = ((0, 256, 0, 256), (256, 256, 128, 256), (512, 256, 256, 384), (768, 128, 384, 256), (896, 256, 512, 256))


def dot(a, b):
    return jnp.dot(a, b, preferred_element_type=F32)


def dot_nt(a, b):
    return lax.dot_general(a, b, (((1,), (1,)), ((), ())), preferred_element_type=F32)


def layer_norm(x):
    mean = jnp.mean(x, -1, keepdims=True)
    centre = x - mean
    var = jnp.mean(centre * centre, -1, keepdims=True)
    return centre * lax.rsqrt(var + 1e-05)


def iota(shape, dim):
    return lax.broadcasted_iota(jnp.int32, shape, dim)


MESH = pl.DeviceIdType.MESH
KEYS = 16 * PAD
PAIR_ROWS = 12
HALF = 8 * PAD
GROUPS = ((0, 256), (256, 512), (768, 384))
WORK = ((1, 0), (0, 0), (1, 1), (1, 2), (0, 1), (0, 2), (1, 3), (0, 3), (0, 4), (1, 4))
PARTS = ((0, 48), (48, 32))


def pair_part(pair_load, pair_ref, mask_ref, weight_ref, table_ref, out, row, col, unroll=24):
    weight_t = weight_ref[...]

    def step(g, carry):
        for n in range(unroll // PAIR_ROWS):
            pair_load(g * (unroll // PAIR_ROWS) + n).wait()
        normed = [layer_norm(pair_ref[g * unroll + u].astype(F32)).astype(BF16) for u in range(unroll)]
        raw = [dot_nt(weight_t, n) for n in normed]
        for u in range(unroll):
            table_ref[pl.ds(g * unroll + u, HEADS, stride=TOK), :TOK] = raw[u]
        return carry

    lax.fori_loop(0, TOK // unroll, step, 0)
    kidx = col * TOK + iota((TOK, TOK), 1)
    qidx = row * TOK + iota((TOK, TOK), 0)
    allowed = (mask_ref[...][None, :] == 1) | (qidx == kidx)
    for h in range(HEADS):
        rows = pl.ds(h * TOK, TOK)
        table_ref[rows, :TOK] = jnp.where(allowed, table_ref[rows, :TOK], -30000.0)
    for n in range(LANES // 128):
        part = table_ref[n * 128 : (n + 1) * 128, :].T[:TOK]
        filled = jnp.concatenate([part, jnp.full((PAD - TOK, 128), NEG, F32)], axis=0)
        out[:, n * 128 : (n + 1) * 128] = filled.astype(BF16)


def atom_project(s, feat_ref, wq, wk, wv, q_ref, k_ref, v_ref):
    for c in range(3):
        normed = layer_norm(feat_ref[s, c * 384 : (c + 1) * 384].astype(F32)).astype(BF16)
        here = pl.ds(RIM + c * 384, 384)
        k_ref[s, here, :] = dot(normed, wk).astype(BF16)
        v_ref[s, here, :CA] = dot(normed, wv).astype(BF16)
        v_ref[s, here, CA:] = jnp.ones((384, CA), BF16)
        q_ref[s, pl.ds(c * 384, 384), :] = dot(normed, wq).astype(BF16)


def atom_rim(s, halo_ref, wk, wv, k_ref, v_ref, row, rows):
    last = RIM + ATOMS
    first_key = k_ref[s, RIM : RIM + 16, :].astype(F32)[:1]
    last_key = k_ref[s, last - 16 : last, :].astype(F32)[15:]
    for side, outside, start, key in ((0, row == 0, 0, first_key), (1, row == rows - 1, last, last_key)):
        normed = layer_norm(halo_ref[side, s].astype(F32)).astype(BF16)
        here = pl.ds(start, RIM)
        k_ref[s, here, :] = jnp.where(outside, jnp.broadcast_to(key, (RIM, CA)), dot(normed, wk)).astype(BF16)
        v_ref[s, here, :CA] = jnp.where(outside, 0.0, dot(normed, wv)).astype(BF16)
        v_ref[s, here, CA:] = jnp.where(outside, 0.0, jnp.ones((RIM, CA), F32)).astype(BF16)


def atom_windows(s, windows, q_ref, k_ref, v_ref, att_ref):
    head_of = iota((AHEADS * QWIN, CA), 0) // QWIN == iota((AHEADS * QWIN, CA), 1) // AHEAD_DIM
    lane_head = iota((QWIN, CA), 1) // AHEAD_DIM
    factor = 1.4426950408889634 / AHEAD_DIM**0.5
    starts = [w * QWIN for w in windows]
    scores = []
    for start in starts:
        q = q_ref[s, pl.ds(start, QWIN), :]
        stacked = jnp.where(head_of, jnp.concatenate([q] * AHEADS, axis=0), jnp.zeros((), BF16))
        scores.append(dot_nt(stacked, k_ref[s, pl.ds(start, KWIN), :]))
    exps = [jnp.exp2((sc - jnp.max(sc, -1, keepdims=True)) * factor).astype(BF16) for sc in scores]
    for start, e in zip(starts, exps):
        both = dot(e, v_ref[s, pl.ds(start, KWIN), :])
        top, low = both[:QWIN, :CA], both[:QWIN, CA:]
        for h in range(1, AHEADS):
            here = slice(h * QWIN, (h + 1) * QWIN)
            top = jnp.where(lane_head == h, both[here, :CA], top)
            low = jnp.where(lane_head == h, both[here, CA:], low)
        att_ref[s, pl.ds(start, QWIN), :] = (top / low).astype(BF16)


def atom_sum(s, chunks, feat_ref, token_ref, wo, agg_ref, att_ref, row):
    total = jnp.zeros((TOK, D), F32)
    for start, size in chunks:
        here = pl.ds(start, size)
        out = (feat_ref[s, here, :].astype(F32) + dot(att_ref[s, here, :], wo)).astype(BF16)
        hidden = jnp.maximum(dot(out, agg_ref[...]), 0.0).astype(BF16)
        onehot = token_ref[start : start + size][None, :] - row * TOK == iota((TOK, size), 0)
        total += dot(onehot.astype(BF16), hidden)
    return total


def token_counts(token_ref, row):
    onehot = token_ref[...][None, :] - row * TOK == iota((TOK, ATOMS), 0)
    return jnp.sum(onehot.astype(F32), -1, keepdims=True)


def token_norm(token_in, gain_ref):
    tnorm = layer_norm(token_in) * gain_ref[...][None, :]
    return jnp.concatenate([tnorm, jnp.zeros((PAD - TOK, D), F32)], axis=0).astype(BF16)


def query_prep(qt_ref, slab, chunk):
    lo, width, clo, cwidth = chunk
    lane = lo + iota((TOK, width), 1)
    fold = (lane % TOK == iota((TOK, width), 0)).astype(BF16)
    own_head = (lo + iota((cwidth, width), 1)) // TOK == (clo + iota((cwidth, width), 0)) // HEAD_DIM
    query = jnp.where(own_head, dot(qt_ref[slab, pl.ds(clo, cwidth), :], fold), 0.0).astype(BF16)
    return fold, own_head, query


def attend(k_ref, vt_ref, bias_of, qt_ref, scores_ref, p_ref, mix_ref, before, after_slab, blk=PAD * 2):
    mix_ref[...] = jnp.zeros_like(mix_ref)
    work = [(slab, CHUNKS[c]) for slab, c in WORK]
    blocks = KEYS // blk
    state = {}
    for i in range(len(work) + 2):
        before(i)
        now = work[i] if i < len(work) else None
        exps = work[i - 1] if 0 <= i - 1 < len(work) else None
        vals = work[i - 2] if i >= 2 else None
        if exps:
            top = jnp.max(state[i - 1][3], axis=0, keepdims=True)
            total = jnp.zeros((8, exps[1][1]), F32)
        if now:
            lo, width, clo, cwidth = now[1]
            state[i] = list(query_prep(qt_ref, *now)) + [jnp.full((8, width), -3e38, F32)]
            ahead = dot(k_ref[0:blk, clo : clo + cwidth], state[i][2])
        if vals:
            _, vwidth, vlo, vcwidth = vals[1]
            out = dot(vt_ref[pl.ds(vlo, vcwidth), :], p_ref[i % 2, :, :vwidth])
        for b in range(blocks):
            here = pl.ds(b * blk, blk)
            if now:
                raw = ahead
                if b + 1 < blocks:
                    ahead = dot(k_ref[(b + 1) * blk : (b + 2) * blk, clo : clo + cwidth], state[i][2])
            if exps:
                ewidth = exps[1][1]
                e = jnp.exp(scores_ref[(i - 1) % 2, here, :ewidth] - top)
                total += jnp.sum(e.reshape(blk // 8, 8, ewidth), axis=0)
                p_ref[(i - 1) % 2, here, :ewidth] = e.astype(BF16)
            if now:
                sc = raw * (1.0 / HEAD_DIM**0.5) + bias_of(now[0], b, blk, lo, width)
                scores_ref[i % 2, here, :width] = sc
                state[i][3] = jnp.maximum(state[i][3], jnp.max(sc.reshape(blk // 8, 8, width), axis=0))
        if exps:
            state[i - 1].append(jnp.sum(total, axis=0, keepdims=True))
        if vals:
            fold, own_head, _, _, vsum = state.pop(i - 2)
            out = jnp.where(own_head, out * (1.0 / vsum), 0.0)
            high = out.astype(BF16)
            rest = (out - high.astype(F32)).astype(BF16)
            mix_ref[vals[0], :, vlo : vlo + vcwidth] += dot_nt(fold, high) + dot_nt(fold, rest)
            if vals[1] == CHUNKS[-1]:
                after_slab(vals[0])


def whole_kernel(mask_ref, pair_w_ref, token_ref, wq, wk, wv, wo, gain_ref, pair_hbm, feat_hbm, agg_hbm,
                 query_hbm, key_hbm, value_hbm, gate_hbm, out_hbm, out_ref,
                 pair_ref, feat_ref, agg_ref, table_ref, halo_ref, q_ref, k_ref, v_ref, att_ref, token_in_ref, counts_ref, give_ref, tall_ref, bias_ref,
                 weights_ref, wvt_ref, keys_ref, vt_ref, qt_ref, sig_ref, scores_ref, p_ref, mix_ref, back_send, back_recv,
                 load_sem, halo_send, halo_recv, bias_send, bias_recv, twin_send, twin_recv, tok_send, tok_recv,
                 pass_send, pass_recv):
    row, col = lax.axis_index("row"), lax.axis_index("sample")
    rows, cols = lax.axis_size("row"), lax.axis_size("sample")
    core, zl, y = row % 2, (row // 2) % 2, row // 4
    x, zh = col % 4, col // 4
    twin, zpair = row + 1 - 2 * core, row + 2 - 4 * zl
    y_up, y_down = (row + 4) % rows, (row + rows - 4) % rows
    r_up, r_down = (row + 1) % rows, (row + rows - 1) % rows
    x_up, x_down = zh * 4 + (x + 1) % 4, zh * 4 + (x + 3) % 4
    z_up, z_down = (col + 4) % cols, (col + cols - 4) % cols
    def pair_load(n):
        here = pl.ds(n * PAIR_ROWS, PAIR_ROWS)
        return pltpu.make_async_copy(pair_hbm.at[here], pair_ref.at[here], load_sem.at[n])

    first = TOK // PAIR_ROWS
    for n in range(first):
        pair_load(n).start()
    sources = [(feat_hbm.at[0], feat_ref.at[0]), (feat_hbm.at[1], feat_ref.at[1]), (agg_hbm, agg_ref)]
    sources += [(source, weights_ref.at[n]) for n, source in enumerate((query_hbm, key_hbm, value_hbm, gate_hbm, out_hbm))]
    loads = [pltpu.make_async_copy(*pair, load_sem.at[first + n]) for n, pair in enumerate(sources)]
    for load in loads:
        load.start()

    barrier = pltpu.get_barrier_semaphore()
    for peer in (twin, zpair, y_up, y_down, r_up, r_down):
        pl.semaphore_signal(barrier, inc=1, device_id=(peer, col), device_id_type=MESH)
    for peer in (x_up, x_down, z_up, z_down):
        pl.semaphore_signal(barrier, inc=1, device_id=(row, peer), device_id_type=MESH)

    sent = []

    def send(src, dst, send_sem, recv_sem, peer_row, peer_col):
        copy = pltpu.make_async_remote_copy(src_ref=src, dst_ref=dst, send_sem=send_sem, recv_sem=recv_sem,
                                            device_id=(peer_row, peer_col), device_id_type=MESH)
        copy.start()
        sent.append(copy)

    def wait(dst, send_sem, recv_sem, peer_row, peer_col):
        pltpu.make_async_remote_copy(src_ref=dst, dst_ref=dst, send_sem=send_sem, recv_sem=recv_sem,
                                     device_id=(peer_row, peer_col), device_id_type=MESH).wait_recv()

    z_order = (zh, (zh + 3) % 4, (zh + 1) % 4, (zh + 2) % 4)

    def slot(g, zb, xb, part):
        rows_here = pl.ds(*part) if part else pl.ds(0, PAD)
        return bias_ref.at[core, xb % 2, zb, xb // 2, rows_here, pl.ds(*GROUPS[g])]

    def got(g, role, zb, xb, part=None):
        n = g * 20 + role
        wait(slot(g, zb, xb, part), bias_send.at[n], bias_recv.at[n], row, col)

    def give(g, role, zb, xb, peer, part=None):
        at, n = slot(g, zb, xb, part), g * 20 + role
        send(at, at, bias_send.at[n], bias_recv.at[n], row, peer)

    def z_own(g):
        give(g, 0, zh, x, z_up)
        give(g, 1, zh, x, z_down)

    def z_pass(g, way):
        got(g, way, z_order[1 + way], x)
        give(g, 2 + way, z_order[1 + way], x, z_down if way else z_up, PARTS[way])

    def z_end(g):
        got(g, 2, z_order[3], x, PARTS[0])
        got(g, 3, z_order[3], x, PARTS[1])

    def x_own(g, j):
        give(g, 4 + 4 * j, z_order[j], x, x_up)
        give(g, 5 + 4 * j, z_order[j], x, x_down)

    def x_pass(g, j, way):
        parts = PARTS if j % 2 else PARTS[::-1]
        origin = (x + 1) % 4 if way else (x + 3) % 4
        got(g, 4 + 4 * j + way, z_order[j], origin)
        give(g, 6 + 4 * j + way, z_order[j], origin, x_down if way else x_up, parts[way])

    def x_end(g, j):
        first, second = PARTS if j % 2 else PARTS[::-1]
        got(g, 6 + 4 * j, z_order[j], (x + 2) % 4, first)
        got(g, 7 + 4 * j, z_order[j], (x + 2) % 4, second)
        at, n = bias_ref.at[core, :, z_order[j], :, :, pl.ds(*GROUPS[g])], g * 4 + j
        send(at, at, twin_send.at[n], twin_recv.at[n], twin, col)

    def twin_end(g):
        for j in range(4):
            n = g * 4 + j
            at = bias_ref.at[1 - core, :, z_order[j], :, :, pl.ds(*GROUPS[g])]
            wait(at, twin_send.at[n], twin_recv.at[n], twin, col)

    def tok_slot(late, yb, zb, part=None):
        at = tall_ref.at[core if late else 1 - core, yb * 2 + zb]
        return at if part is None else at.at[pl.ds(*part)]

    def tok_wait(late, role, yb, zb, part=None):
        n = late * 9 + role
        wait(tok_slot(late, yb, zb, part), tok_send.at[n], tok_recv.at[n], row, col)

    def tok_give(late, role, yb, zb, peer, part=None):
        at, n = tok_slot(late, yb, zb, part), late * 9 + role
        send(at, at, tok_send.at[n], tok_recv.at[n], peer, col)

    zs = (zl, 1 - zl)

    def tok_own(late):
        tok_give(late, 0, y, zl, zpair)
        tok_give(late, 1, y, zl, y_up)
        tok_give(late, 2, y, zl, y_down)

    def tok_second(late):
        tok_wait(late, 0, y, 1 - zl)
        tok_give(late, 5, y, 1 - zl, y_up)
        tok_give(late, 6, y, 1 - zl, y_down)

    def tok_pass(late, j, way):
        origin = (y + 1) % 4 if way else (y + 3) % 4
        tok_wait(late, 1 + 4 * j + way, origin, zs[j])
        tok_give(late, 3 + 4 * j + way, origin, zs[j], y_down if way else y_up, PARTS[way])

    def tok_end(late):
        for j in range(2):
            tok_wait(late, 3 + 4 * j, (y + 2) % 4, zs[j], PARTS[0])
            tok_wait(late, 4 + 4 * j, (y + 2) % 4, zs[j], PARTS[1])

    def windows(s, which):
        atom_windows(s, which, q_ref, k_ref, v_ref, att_ref)

    def inner(s):
        token_in_ref[s] = atom_sum(s, ((128, 384), (512, 384), (896, 128)), feat_ref, token_ref, wo[...], agg_ref, att_ref,
                                   row)

    def tokens(s):
        edges = atom_sum(s, ((0, 128), (1024, 128)), feat_ref, token_ref, wo[...], agg_ref, att_ref, row)
        token_in = (token_in_ref[s] + edges) / counts_ref[:, :1]
        token_in_ref[s] = token_in
        return token_norm(token_in, gain_ref)

    def rim(s):
        atom_rim(s, halo_ref, wk[...], wv[...], k_ref, v_ref, row, rows)
        windows(s, (0, 1, ATOMS // QWIN - 2, ATOMS // QWIN - 1))

    pair_part(pair_load, pair_ref, mask_ref, pair_w_ref, table_ref, bias_ref.at[core, x % 2, zh, x // 2], row, col)
    loads[0].wait()
    loads[1].wait()

    def inside(s):
        atom_project(s, feat_ref, wq[...], wk[...], wv[...], q_ref, k_ref, v_ref)
        for lo, hi in ((2, 14), (14, 26), (26, 34)):
            windows(s, range(lo, hi))

    inside(1 - core)

    pl.semaphore_wait(barrier, 10)
    send(feat_hbm.at[:, ATOMS - RIM :], halo_ref.at[0], halo_send.at[0], halo_recv.at[0], r_up, col)
    send(feat_hbm.at[:, :RIM], halo_ref.at[1], halo_send.at[1], halo_recv.at[1], r_down, col)

    def project_tokens(which):
        base = pl.multiple_of(which * HALF, HALF)
        block = tall_ref[which].reshape(HALF, D)
        keys_ref[pl.ds(base, HALF), :] = dot(block, weights_ref[1]).astype(BF16)
        vt_ref[:, pl.ds(base, HALF)] = dot_nt(wvt_ref[...], block).astype(BF16)

    z_own(0)
    x_own(0, 0)
    z_own(1)
    x_own(1, 0)
    inside(core)
    counts_ref[...] = jnp.broadcast_to(token_counts(token_ref, row), (TOK, 128))
    loads[2].wait()
    inner(1 - core)
    inner(core)
    for load in loads[3:]:
        load.wait()
    wvt_ref[...] = weights_ref[2].astype(F32).T.astype(BF16)
    x_own(2, 0)
    wait(halo_ref.at[0], halo_send.at[0], halo_recv.at[0], r_up, col)
    wait(halo_ref.at[1], halo_send.at[1], halo_recv.at[1], r_down, col)
    rim(1 - core)
    x_pass(0, 0, 0)
    x_pass(0, 0, 1)
    give_ref[...] = tokens(1 - core)
    send(give_ref, tall_ref.at[core, y * 2 + zl], pass_send.at[0], pass_recv.at[0], twin, col)
    rim(core)
    tall_ref[core, y * 2 + zl] = tokens(core)
    tok_own(1)
    z_pass(0, 0)
    z_pass(0, 1)
    wait(tall_ref.at[1 - core, y * 2 + zl], pass_send.at[0], pass_recv.at[0], twin, col)
    tok_own(0)
    x_own(0, 1)
    for slab in range(2):
        block = tall_ref[core if slab else 1 - core, y * 2 + zl]
        qt_ref[slab] = dot(block, weights_ref[0])[:TOK].T.astype(BF16)
        sig_ref[slab] = jax.nn.sigmoid(dot(block, weights_ref[3])[:TOK])
    x_own(0, 2)
    x_pass(1, 0, 0)
    x_pass(1, 0, 1)
    x_pass(2, 0, 0)
    x_pass(2, 0, 1)
    x_end(0, 0)
    z_pass(1, 0)
    z_pass(1, 1)
    x_pass(0, 1, 0)
    x_pass(0, 1, 1)
    x_own(1, 1)
    tok_pass(1, 0, 0)
    tok_pass(1, 0, 1)
    tok_second(1)
    x_pass(0, 2, 0)
    x_pass(0, 2, 1)
    x_end(1, 0)
    x_own(1, 2)
    x_end(2, 0)
    x_end(0, 1)
    tok_pass(0, 0, 0)
    tok_pass(0, 0, 1)
    z_own(2)
    z_end(0)
    x_own(0, 3)
    tok_second(0)
    x_pass(1, 1, 0)
    x_pass(1, 1, 1)
    x_end(0, 2)
    tok_pass(1, 1, 1)
    x_pass(1, 2, 0)
    tok_pass(1, 1, 0)
    x_pass(1, 2, 1)
    x_pass(0, 3, 0)
    z_end(1)
    x_own(1, 3)
    x_pass(0, 3, 1)
    x_end(1, 1)
    z_pass(2, 1)
    z_pass(2, 0)
    x_own(2, 1)
    tok_pass(0, 1, 1)
    x_end(1, 2)
    tok_pass(0, 1, 0)
    x_own(2, 2)
    x_pass(1, 3, 0)
    x_pass(1, 3, 1)
    x_end(0, 3)
    x_pass(2, 1, 0)
    x_pass(2, 1, 1)
    z_end(2)
    x_own(2, 3)
    tok_end(0)
    project_tokens(1 - core)
    x_end(1, 3)
    x_pass(2, 2, 0)
    x_pass(2, 2, 1)
    tok_end(1)
    project_tokens(core)
    x_end(2, 1)
    x_pass(2, 3, 0)
    x_pass(2, 3, 1)

    def before(i):
        if i == 1:
            twin_end(0)
        if i == 2:
            x_end(2, 2)
        if i == 4:
            x_end(2, 3)
            twin_end(1)
        if i == 7:
            twin_end(2)

    def bias_of(slab, b, blk, lo, width):
        first = b * (blk // PAD)
        at = bias_ref[core if slab else 1 - core, first // 8, first % 8 // 2, :, :, lo : lo + width]
        return at.astype(F32).reshape(blk, width)

    def after_slab(slab):
        gated = mix_ref[slab] * sig_ref[slab]
        if slab == 0:
            back_send[...] = jnp.concatenate([gated, jnp.zeros((PAD - TOK, D), F32)], axis=0).astype(BF16)
            send(back_send, back_recv, pass_send.at[1], pass_recv.at[1], twin, col)
        else:
            out_ref[core] = (token_in_ref[core] + dot(gated.astype(BF16), weights_ref[4])).astype(BF16)

    attend(keys_ref, vt_ref, bias_of, qt_ref, scores_ref, p_ref, mix_ref, before, after_slab)
    wait(back_recv, pass_send.at[1], pass_recv.at[1], twin, col)
    out_ref[1 - core] = (token_in_ref[1 - core] + dot(back_recv[...], weights_ref[4])[:TOK]).astype(BF16)
    for copy in sent:
        copy.wait_send()


def shards(atom_feat, atom_token, pair_cond, token_mask, atom_wq, atom_wk, atom_wv, atom_wo, agg_weight, pair_weight,
           token_gain, query_weight, key_weight, value_weight, gate_weight, out_weight):
    whole = ATOMS + 2 * RIM
    dma = pltpu.SemaphoreType.DMA
    here, there = pl.BlockSpec(memory_space=pltpu.VMEM), pl.BlockSpec(memory_space=pl.ANY)
    return pl.pallas_call(
        whole_kernel,
        out_shape=jax.ShapeDtypeStruct((2, TOK, D), BF16),
        in_specs=[here] * 8 + [there] * 8,
        out_specs=here,
        scratch_shapes=[
            pltpu.VMEM((TOK, TOK, 128), BF16), pltpu.VMEM((2, ATOMS, CA), BF16), pltpu.VMEM((CA, D), BF16),
            pltpu.VMEM((LANES, 128), F32), pltpu.VMEM((2, 2, RIM, CA), BF16),
            pltpu.VMEM((2, ATOMS, CA), BF16), pltpu.VMEM((2, whole, CA), BF16), pltpu.VMEM((2, whole, 2 * CA), BF16),
            pltpu.VMEM((2, ATOMS, CA), BF16), pltpu.VMEM((2, TOK, D), F32), pltpu.VMEM((TOK, 128), F32), pltpu.VMEM((PAD, D), BF16),
            pltpu.VMEM((2, 8, PAD, D), BF16), pltpu.VMEM((2, 2, 4, 2, PAD, LANES), BF16), pltpu.VMEM((5, D, D), BF16),
            pltpu.VMEM((D, D), BF16), pltpu.VMEM((KEYS, D), BF16), pltpu.VMEM((D, KEYS), BF16),
            pltpu.VMEM((2, D, TOK), BF16), pltpu.VMEM((2, TOK, D), F32), pltpu.VMEM((2, KEYS, 256), F32),
            pltpu.VMEM((2, KEYS, 256), BF16), pltpu.VMEM((2, TOK, D), F32), pltpu.VMEM((PAD, D), BF16),
            pltpu.VMEM((PAD, D), BF16), dma((14,)), dma((2,)), dma((2,)), dma((60,)), dma((60,)), dma((12,)), dma((12,)),
            dma((18,)), dma((18,)), dma((2,)), dma((2,)),
        ],
        compiler_params=pltpu.CompilerParams(collective_id=0, has_side_effects=True, vmem_limit_bytes=60 * 1024 * 1024),
        name="whole",
    )(token_mask, pair_weight.T, atom_token, atom_wq, atom_wk, atom_wv, atom_wo, token_gain, pair_cond, atom_feat,
      agg_weight, query_weight, key_weight, value_weight, gate_weight, out_weight)


def solution(mesh):
    placed = (P("sample", "row", None), P("row"), P("row", "sample", None), P("sample")) + (P(),) * 12
    return jax.shard_map(shards, mesh=mesh, in_specs=placed, out_specs=P("sample", "row", None), check_vma=False)
```
